256 devices in a mesh: grp: 32 (over y, x, core), bal: 8 (over z).
Axes of the slice: x: 4, y: 4, z: 8, core: 2. Of those that a mesh axis runs over, the one named last changes fastest.
Arguments:
- grad_out: float32 [32768, 256], P(('grp', 'bal')), may hold values from -6 to 6
- deriv_mask: int32 [32768, 256], P(('grp', 'bal')), may hold values 0 or 1
- weight: float32 [256, 256], replicated, may hold values from -0.375 to 0.375
- zcache: float32 [32768, 256], P(('grp', 'bal')), may hold values from -0.03125 to 0.03125
- tile_values: float32 [8192, 128, 128], P(('grp', 'bal')), may hold values from -0.09375 to 0.09375
- tile_source: int32 [8192], P(('grp', 'bal')), may hold values from 0 to 7
- tile_slot: int32 [8192], P(('grp', 'bal')), may hold values from 0 to 63, as said below
- recv_target: int32 [16384], P(('grp', 'bal')), may hold values from -1 to 7, as said below
Outputs:
- weight_grad: float32 [256, 256], replicated
- fixed_grad: float32 [32768, 256], P(('grp', 'bal'))
The draws below stay inside these ranges and needn't reach their ends.
Inputs may be any that keep to these rules, and one draw needn't show every extreme that they name: Each device's tile_slot values are distinct, so at most 2 tiles go from one device to one row group; every device fills all 2 slots toward some row group. recv_target is -1 exactly at the slots that no tile_slot of the sending device names, and a block index within the row group elsewhere.
All inputs are finite; a program needn't handle non-finite values. No bound on the sum of `deriv_mask` on one device may be relied on, other than what follows from the above.
Results may differ from the reference program's by a relative error of at most 0.0001.
Values sent between devices are 32-bit elements; how exact they have to be, the bound alone decides.
No kernel may reach another device: no remote copies, remote signals or barrier semaphores. Data moves between devices by JAX's collectives and lax.ppermute only.
A program may use at most 128 MiB of HBM per device.

```python
import jax
import jax.numpy as jnp
from jax import lax

F = 256
BLK = 128
RB = 1
TPD = 32
STEPS = 3
CAP = 2
NODES = 32768
N_GRP = 32
N_BAL = 8


def routing_tables(key):
    base = jax.random.fold_in(key, 101)
    devices = N_GRP * N_BAL
    slots = N_GRP * CAP
    first, second, third = jax.random.split(base, 3)
    full_group = jax.random.randint(first, (devices,), 0, N_GRP)
    noise = jax.random.randint(second, (devices, slots), 0, 2 ** 20)
    slot_ids = jnp.arange(slots, dtype=jnp.int32)
    forced = (slot_ids[None, :] // CAP == full_group[:, None]).astype(jnp.int32)
    scores = noise * slots + slot_ids[None, :] - forced * 2 ** 28
    order = jnp.argsort(scores, axis=1, stable=True).astype(jnp.int32)
    tile_slot = order[:, :TPD]
    targets = jax.random.randint(third, (devices, TPD), 0, RB * N_BAL)
    rows = jnp.arange(devices, dtype=jnp.int32)[:, None]
    table = jnp.full((devices, slots), -1, jnp.int32).at[rows, tile_slot].set(targets.astype(jnp.int32))
    table = table.reshape(N_GRP, N_BAL, N_GRP, CAP).transpose(2, 1, 0, 3).reshape(-1)
    return (tile_slot.reshape(-1), table)


def draw_tile_slot(key, part):
    return routing_tables(key)[0]


def draw_recv_target(key, part):
    return routing_tables(key)[1]


def with_ends(values, rng, least, top_value):
    shape = values.shape
    index_at = [jax.random.randint(jax.random.fold_in(rng, axis), (), 0, shape[axis]) for axis in range(len(shape))]
    values = values.at[tuple(index_at)].set(least)
    longest = shape.index(max(shape))
    index_at[longest] = (index_at[longest] + 1) % shape[longest]
    return values.at[tuple(index_at)].set(top_value)


def levels(rng, shape, pieces, low, largest):
    gain, own = 1.0, jax.random.fold_in(rng, 6)
    for dim, shards_of in pieces:
        steps = jnp.exp(jax.random.uniform(jax.random.fold_in(own, dim), (shards_of,), jnp.float32, low / len(pieces), largest / len(pieces)))
        gain = gain * jnp.repeat(steps, shape[dim] // shards_of).reshape([-1 if axis == dim else 1 for axis in range(len(shape))])
    return gain


def centred(rng, extent, scale, bound, cuts=(), kind=jnp.bfloat16):
    level = levels(rng, extent, cuts, -0.22, 0.18) if cuts else 1.0
    values = jax.random.normal(rng, extent, jnp.float32) * scale * level
    return jnp.minimum(jnp.maximum(values, -bound), bound).astype(kind)


def setup_inputs(seed: int = 0) -> dict:
    arg_keys = jax.random.split(jax.random.key(seed), 9)
    grad_out = centred(arg_keys[0], (NODES, F), 1.0, 6.0, ((0, 256),), jnp.float32)
    deriv_mask = with_ends((jax.random.randint(arg_keys[1], (NODES, F), 0, 2) < 1).astype(jnp.int32), jax.random.fold_in(arg_keys[1], 1), 0, 1)
    weight = centred(arg_keys[2], (F, F), F ** -0.5, 0.375, (), jnp.float32)
    zcache = centred(arg_keys[3], (NODES, F), NODES ** -0.5, 0.03125, ((0, 256),), jnp.float32)
    tile_values = centred(arg_keys[4], (N_GRP * N_BAL * TPD, BLK, BLK), (BLK * TPD // RB) ** -0.5, 0.09375, ((0, 256),), jnp.float32)
    tile_source = with_ends(jax.random.randint(arg_keys[5], (N_GRP * N_BAL * TPD,), 0, RB * N_BAL), jax.random.fold_in(arg_keys[5], 1), 0, (RB * N_BAL) - 1).astype(jnp.int32)
    tile_slot = draw_tile_slot(jax.random.fold_in(arg_keys[8], 71), 0)
    recv_target = draw_recv_target(jax.random.fold_in(arg_keys[8], 71), 0)
    return {"grad_out": grad_out, "deriv_mask": deriv_mask, "weight": weight, "zcache": zcache, "tile_values": tile_values, "tile_source": tile_source, "tile_slot": tile_slot, "recv_target": recv_target}


def sparse_apply(grad, tile_values, source_block, dest_block):
    blocks = grad.reshape(NODES // BLK, BLK, F)
    devices = N_GRP * N_BAL

    def one_device(index, total):
        tiles = lax.dynamic_slice_in_dim(tile_values, index * TPD, TPD, 0)
        sources = lax.dynamic_slice_in_dim(source_block, index * TPD, TPD, 0)
        dests = lax.dynamic_slice_in_dim(dest_block, index * TPD, TPD, 0)
        partial_value = jnp.einsum("tij,tjf->tif", tiles, blocks[sources], precision=lax.Precision.HIGHEST)
        return total.at[dests].add(partial_value)

    start = jnp.zeros((NODES // BLK, BLK, F), jnp.float32)
    total = lax.fori_loop(0, devices, one_device, start)
    return total.reshape(NODES, F)


def reference(grad_out, deriv_mask, weight, zcache, tile_values, tile_source, tile_slot, recv_target):
    per_group = RB * N_BAL
    device = jnp.arange(N_GRP * N_BAL * TPD, dtype=jnp.int32) // TPD
    group_of = device // N_BAL
    bal_of = device % N_BAL
    dest_group = tile_slot // CAP
    place = tile_slot % CAP
    recv_index = (dest_group * N_BAL + bal_of) * (N_GRP * CAP) + group_of * CAP + place
    target = recv_target[recv_index]
    source_block = (group_of * per_group + tile_source).astype(jnp.int32)
    dest_block = (dest_group * per_group + target).astype(jnp.int32)
    mask_float = deriv_mask.astype(jnp.float32)
    fixed_grad = grad_out
    for step in range(STEPS):
        summed = sparse_apply(fixed_grad, tile_values, source_block, dest_block)
        product = jnp.dot(summed, weight, precision=lax.Precision.HIGHEST, preferred_element_type=jnp.float32)
        fixed_grad = mask_float * product + grad_out
    weight_grad = jnp.dot(fixed_grad.T, zcache, precision=lax.Precision.HIGHEST, preferred_element_type=jnp.float32)
    return weight_grad, fixed_grad
```

```python
import functools

import jax
import jax.numpy as jnp
from jax import lax
from jax.experimental import pallas as pl
from jax.experimental.pallas import tpu as pltpu
from jax.sharding import Mesh
from jax.sharding import PartitionSpec as P

STEPS = 3
BLK = 128
BUFS = 8
PLANE = ("y", "x")
GRP = ("y", "x", "core")
ALL = ("y", "x", "core", "bal")
HIGHEST = lax.Precision.HIGHEST


def split(value):
    high = value.astype(jnp.bfloat16)
    low = (value - high.astype(jnp.float32)).astype(jnp.bfloat16)
    return high, low


def products_kernel(count, place, source, target, *refs):
    n_blocks = len(refs) - 6
    blocks = refs[:n_blocks]
    tiles, keep, send, rhs, held, sems = refs[n_blocks:]
    chips = keep.shape[0] // BLK
    total = count[0]

    def copy(k, slot):
        return pltpu.make_async_copy(tiles.at[place[k]], held.at[slot], sems.at[slot])

    for slot in range(BUFS):

        @pl.when(slot < total)
        def _(slot=slot):
            copy(slot, slot).start()

    for i, block in enumerate(blocks):
        high, low = split(block[...])
        rhs[i, 0:BLK] = high
        rhs[i, BLK : 2 * BLK] = high
        rhs[i, 2 * BLK : 3 * BLK] = low
    keep[...] = jnp.zeros_like(keep)
    send[...] = jnp.zeros_like(send)

    def body(k, carry):
        slot = lax.rem(k, BUFS)
        copy(k, slot).wait()
        high, low = split(held[slot])
        lhs = jnp.concatenate([high, low, high], axis=1)
        product = jnp.dot(lhs, rhs[source[k]], preferred_element_type=jnp.float32)
        where = target[k]
        rows = pl.ds(pl.multiple_of(lax.rem(where, chips) * BLK, BLK), BLK)

        @pl.when(where < chips)
        def _():
            keep[rows] += product

        @pl.when(where >= chips)
        def _():
            send[rows] += product

        @pl.when(k + BUFS < total)
        def _():
            copy(k + BUFS, slot).start()

        return carry

    lax.fori_loop(0, total, body, 0)


def products(count, place, source, target, blocks, tiles, chips):
    width = blocks[0].shape[1]
    smem = pl.BlockSpec(memory_space=pltpu.SMEM)
    vmem = pl.BlockSpec(memory_space=pltpu.VMEM)
    out = jax.ShapeDtypeStruct((chips * BLK, width), jnp.float32)
    return pl.pallas_call(
        products_kernel,
        out_shape=(out, out),
        in_specs=[smem] * 4 + [vmem] * len(blocks) + [pl.BlockSpec(memory_space=pl.ANY)],
        out_specs=(vmem, vmem),
        scratch_shapes=[
            pltpu.VMEM((len(blocks), 3 * BLK, width), jnp.bfloat16),
            pltpu.VMEM((BUFS, BLK, BLK), jnp.float32),
            pltpu.SemaphoreType.DMA((BUFS,)),
        ],
        compiler_params=pltpu.CompilerParams(vmem_limit_bytes=32 * 2**20),
        cost_estimate=pl.CostEstimate(
            flops=32 * 3 * 2 * BLK * BLK * width, bytes_accessed=8 * 2**20, transcendentals=0
        ),
    )(count, place, source, target, *blocks, tiles)


def shift(value, axis, by):
    n = lax.axis_size(axis)
    return lax.ppermute(value, axis, [(i, (i + by) % n) for i in range(n)])


def ring_gather(value):
    n = lax.axis_size("bal")
    found = [value] + [None] * (n - 1)
    ahead = behind = value
    for hop in range(1, n // 2 + 1):
        ahead = shift(ahead, "bal", 1)
        found[hop] = ahead
        if n - hop > hop:
            behind = shift(behind, "bal", -1)
            found[n - hop] = behind
    return found


def spread(value, axes):
    return lax.all_to_all(value, axes, split_axis=0, concat_axis=0, tiled=True)


def summed_everywhere(term):
    rows, width = term.shape
    half = rows // 2
    core = lax.axis_index("core")
    mine = lax.dynamic_slice_in_dim(term, core * half, half, 0)
    other = lax.dynamic_slice_in_dim(term, (1 - core) * half, half, 0)
    mine = mine + shift(other, "core", 1)
    chips = ("y", "x", "bal")
    n = lax.axis_size(chips)
    row = spread(mine, chips).reshape(n, half // n, width).sum(0)
    back = jnp.broadcast_to(row[None], (n, half // n, width)).reshape(half, width)
    mine = spread(back, chips)
    other = shift(mine, "core", 1)
    first = jnp.where(core == 0, mine, other)
    second = jnp.where(core == 0, other, mine)
    return jnp.concatenate([first, second], axis=0)


def per_device(
    grad_out, deriv_mask, weight, zcache, tile_values, tile_source, tile_slot, recv_target
):
    rows, width = grad_out.shape
    n_bal = lax.axis_size("bal")
    chips = lax.axis_size(PLANE)
    bal = lax.axis_index("bal")
    core = lax.axis_index("core")

    tiles = lax.all_gather(tile_values, "bal", axis=0, tiled=True)
    wanted = spread(recv_target, GRP)
    code = (tile_slot // 2) * 64 + wanted[tile_slot] * 8 + tile_source
    per = code.shape[0]
    codes = spread(jnp.broadcast_to(code[None], (n_bal, per)).reshape(-1), "bal")
    group, block, source = codes // 64, (codes // 8) % 8, codes % 8
    chosen = block == bal
    n = codes.shape[0]
    order = jnp.arange(n, dtype=jnp.int32)
    rank = jnp.sum(jnp.where(chosen[None, :] & (order[None, :] < order[:, None]), 1, 0), axis=1)
    hit = (chosen & (order < n))[None, :] & (rank[None, :] == order[:, None])

    def pick(value):
        return jnp.sum(jnp.where(hit, value[None, :], 0), axis=1)

    count = jnp.sum(chosen.astype(jnp.int32)).reshape(1)
    place = pick(order)
    behind = pick((bal - source) % n_bal)
    target = pick(group // 2 + chips * ((group % 2) ^ core))

    mask_float = deriv_mask.astype(jnp.float32)
    fixed_grad = grad_out
    for step in range(STEPS):
        blocks = ring_gather(fixed_grad)
        keep, send = products(count, place, behind, target, blocks, tiles, chips)
        partial_sum = keep + shift(send, "core", 1)
        owned = spread(partial_sum, PLANE).reshape(chips, rows, width).sum(0)
        product = jnp.dot(owned, weight, precision=HIGHEST, preferred_element_type=jnp.float32)
        fixed_grad = mask_float * product + grad_out
    local_term = jnp.dot(
        fixed_grad.T, zcache, precision=HIGHEST, preferred_element_type=jnp.float32
    )
    return (summed_everywhere(local_term), fixed_grad)


def solution(mesh):
    fine = Mesh(mesh.devices.reshape(4, 4, 2, mesh.shape["bal"]), ALL)
    in_specs = (
        P(ALL, None),
        P(ALL, None),
        P(),
        P(ALL, None),
        P(ALL, None, None),
        P(ALL),
        P(ALL),
        P(ALL),
    )
    out_specs = (P(), P(ALL, None))
    return jax.shard_map(
        per_device, mesh=fine, in_specs=in_specs, out_specs=out_specs, check_vma=False
    )
```

```python
import functools

import jax
import jax.numpy as jnp
from jax import lax
from jax.experimental import pallas as pl
from jax.experimental.pallas import tpu as pltpu
from jax.sharding import Mesh
from jax.sharding import PartitionSpec as P

STEPS = 3
BLK = 128
UNROLL = 4
RING, HOPS, FACTS = 8, 4, 8
PIECES = (16, 6, 4)
CAPS = (26, 22, 16, 7)
HELD = 64
PLANE = ("y", "x")
GRP = ("y", "x", "core")
ALL = ("y", "x", "core", "bal")
HIGHEST = lax.Precision.HIGHEST


def split(value):
    high = value.astype(jnp.bfloat16)
    low = (value - high.astype(jnp.float32)).astype(jnp.bfloat16)
    return high, low


def pack_kernel(here, tgt, tile_slot, tile_source, tiles, facts, *refs):
    pieces, (order, at, sems) = refs[:-3], refs[-3:]
    n_tiles = tile_slot.shape[0]
    n_sent = sum(PIECES)
    room = n_tiles + 1

    for way in range(RING + 1):
        at[way] = 0

    def way_of(j):
        return (facts[1, j] - here[0] + RING) & (RING - 1)

    def count(j, carry):
        s = tile_slot[j]
        facts[0, j] = s >> 1
        facts[1, j] = tgt[s >> 1, s & 1]
        facts[2, j] = tile_source[j]
        way = way_of(j)
        at[way] = at[way] + 1
        return carry

    lax.fori_loop(0, n_tiles, count, 0)
    both = at[HOPS]
    ahead, behind = (both + 1) >> 1, room + (both >> 1)
    at[HOPS] = 0
    at[RING] = room
    for hops in range(HOPS - 1, 0, -1):
        found = at[hops], at[RING - hops]
        at[hops], at[RING - hops] = ahead, behind
        ahead, behind = ahead + found[0], behind + found[1]
    at[0] = 0
    for k in range(n_sent):
        order[k] = 0
        order[room + k] = 0

    def place(j, turn):
        way = way_of(j)
        opposite = (way == HOPS).astype(jnp.int32)
        way = way + HOPS * (opposite & turn)
        where = at[way]
        at[way] = where + 1
        order[jnp.where(way == 0, 2 * room, where)] = j
        return turn ^ opposite

    lax.fori_loop(0, n_tiles, place, jnp.int32(0))

    copies = []
    for side in range(2):
        k = 0
        for piece in pieces[side * len(PIECES) : (side + 1) * len(PIECES)]:
            for i in range(piece.shape[0] // BLK):
                copies.append(
                    pltpu.make_async_copy(
                        tiles.at[order[side * room + k]],
                        piece.at[pl.ds(i * BLK, BLK)],
                        sems.at[side * n_sent + k],
                    )
                )
                k += 1
    for copy in copies:
        copy.start()
    for copy in copies:
        copy.wait()


def pack(bal, tgt, tile_slot, tile_source, tiles):
    smem = pl.BlockSpec(memory_space=pltpu.SMEM)
    vmem = pl.BlockSpec(memory_space=pltpu.VMEM)
    out = [jax.ShapeDtypeStruct((size * BLK, BLK), jnp.float32) for size in PIECES] * 2
    facts, *pieces = pl.pallas_call(
        pack_kernel,
        out_shape=[jax.ShapeDtypeStruct((FACTS, BLK), jnp.int32)] + out,
        in_specs=[smem] * 4 + [pl.BlockSpec(memory_space=pl.ANY)],
        out_specs=[smem] + [vmem] * len(out),
        scratch_shapes=[
            pltpu.SMEM((2 * tile_slot.shape[0] + 3,), jnp.int32),
            pltpu.SMEM((RING + 1,), jnp.int32),
            pltpu.SemaphoreType.DMA((2 * sum(PIECES),)),
        ],
        compiler_params=pltpu.CompilerParams(vmem_limit_bytes=8 * 2**20),
    )(bal.reshape(1), tgt, tile_slot, tile_source, tiles)
    return facts, list(pieces[: len(PIECES)]), list(pieces[len(PIECES) :])


SOURCE, TARGET, OWN, ENDS, FIRST = 0, HELD + 1, 2 * (HELD + 1), 3 * (HELD + 1), 4 * (HELD + 1)
COUNT, TOO_MANY, LISTED = 5 * (HELD + 1), 5 * (HELD + 1) + 1, 5 * (HELD + 1) + 2


def routes():
    ahead = [(h, h, 0) for h in range(1, HOPS + 1)]
    behind = [(RING - h, h, 1) for h in range(HOPS, 0, -1)]
    return ahead + behind


def list_kernel(chips, per, here, facts, plan):
    bal, core = here[0], here[1]
    cut = [sum(PIECES[:i]) for i in range(len(PIECES) + 1)]

    def clear(k, carry):
        plan[SOURCE + k] = 0
        return carry

    lax.fori_loop(0, HELD + 1, clear, 0)

    def sender(row):
        return ((bal - row + RING) & (RING - 1)) * FACTS

    def note(k, row, j):
        at = jnp.minimum(k, HELD)
        group = facts[sender(row), j]
        plan[SOURCE + at] = (bal - facts[sender(row) + 2, j] + RING) & (RING - 1)
        plan[TARGET + at] = (group >> 1) + chips * ((group & 1) ^ core)
        plan[OWN + at] = j

    def way(row, j):
        return (facts[sender(row) + 1, j] - bal + row + RING) & (RING - 1)

    def own(j, k):
        note(k, 0, j)
        return k + (way(0, j) == 0).astype(jnp.int32)

    total = lax.fori_loop(0, per, own, jnp.int32(0))
    plan[ENDS] = jnp.minimum(total, HELD)
    plan[FIRST] = 0
    too_many = jnp.int32(0)
    index = 1
    for row, hops, side in routes():

        def one(j, carry, row=row, hops=hops, side=side):
            k, farther, opposite = carry
            d = way(row, j)
            note(k, row, j)
            is_opposite = d == HOPS
            if hops == HOPS:
                mine = is_opposite & ((opposite & 1) == side)
                far = jnp.int32(0)
            else:
                mine = d == row
                if side == 0:
                    far = ((d > row) & (d < HOPS)).astype(jnp.int32)
                else:
                    far = ((d < row) & (d > HOPS)).astype(jnp.int32)
            return (
                k + mine.astype(jnp.int32),
                farther + far,
                opposite + is_opposite.astype(jnp.int32),
            )

        stop, farther, opposite = lax.fori_loop(
            0, per, one, (total, jnp.int32(0), jnp.int32(0))
        )
        if hops < HOPS:
            farther = farther + ((opposite + 1 - side) >> 1)
        first, last = farther, farther + stop - total
        too_many = jnp.where(last > CAPS[hops - 1], 1, too_many)
        for i in range(len(PIECES)):
            size = min(cut[i + 1], CAPS[hops - 1]) - cut[i]
            if size <= 0:
                break
            begin = jnp.clip(first, cut[i], cut[i] + size)
            end = jnp.clip(last, cut[i], cut[i] + size)
            total = total + end - begin
            plan[ENDS + index] = jnp.minimum(total, HELD)
            plan[FIRST + index] = begin - cut[i]
            index += 1
    plan[COUNT] = jnp.minimum(total, HELD)
    plan[TOO_MANY] = jnp.where(total > HELD, 1, too_many)

    def pad(k, carry):
        plan[TARGET + k] = 2 * chips
        return carry

    lax.fori_loop(jnp.minimum(total, HELD), HELD + 1, pad, 0)


def make_list(chips, per, here, facts):
    smem = pl.BlockSpec(memory_space=pltpu.SMEM)
    return pl.pallas_call(
        functools.partial(list_kernel, chips, per),
        out_shape=jax.ShapeDtypeStruct((LISTED,), jnp.int32),
        in_specs=[smem, smem],
        out_specs=smem,
    )(here, facts)


def collect_kernel(plan, *refs):
    buffers, (out, held, sems) = refs[:-3], refs[-3:]

    def copy(buffer, k, where):
        rows = pl.ds(pl.multiple_of(where * BLK, BLK), BLK)
        return pltpu.make_async_copy(buffer.at[rows], held.at[k], sems.at[k])

    for i, buffer in enumerate(buffers):
        start = 0 if i == 0 else plan[ENDS + i - 1]
        first = plan[FIRST + i]

        def begin(k, carry, i=i, buffer=buffer, start=start, first=first):
            copy(buffer, k, plan[OWN + k] if i == 0 else first + k - start).start()
            return carry

        lax.fori_loop(start, plan[ENDS + i], begin, 0)

    def finish(k, carry):
        copy(buffers[0], k, 0).wait()
        high, low = split(held[k])
        out[k] = jnp.concatenate([high, low], axis=1)
        return carry

    lax.fori_loop(0, plan[COUNT], finish, 0)


def collect(plan, buffers):
    smem = pl.BlockSpec(memory_space=pltpu.SMEM)
    return pl.pallas_call(
        collect_kernel,
        out_shape=jax.ShapeDtypeStruct((HELD, BLK, 2 * BLK), jnp.bfloat16),
        in_specs=[smem] + [pl.BlockSpec(memory_space=pl.ANY)] * len(buffers),
        out_specs=pl.BlockSpec(memory_space=pltpu.VMEM),
        scratch_shapes=[
            pltpu.VMEM((HELD, BLK, BLK), jnp.float32),
            pltpu.SemaphoreType.DMA((HELD,)),
        ],
        compiler_params=pltpu.CompilerParams(vmem_limit_bytes=16 * 2**20),
    )(plan, *buffers)


def products_kernel(plan, *refs):
    n_blocks = len(refs) - 3
    blocks = refs[:n_blocks]
    tiles, out, rhs = refs[n_blocks:]
    for i, block in enumerate(blocks):
        high, low = split(block[0:BLK])
        rhs[i, 0:BLK] = high
        rhs[i, BLK : 2 * BLK] = high
        rhs[i, 2 * BLK : 3 * BLK] = low
    out[...] = jnp.zeros_like(out)

    def body(turn, carry):
        first = turn * UNROLL
        found = []
        for k in range(UNROLL):
            tile = tiles[first + k]
            lhs = jnp.concatenate([tile, tile[:, :BLK]], axis=1)
            found.append(
                jnp.dot(lhs, rhs[plan[SOURCE + first + k]], preferred_element_type=jnp.float32)
            )
        for k in range(UNROLL):
            rows = pl.ds(pl.multiple_of(plan[TARGET + first + k] * BLK, BLK), BLK)
            out[rows] += found[k]
        return carry

    lax.fori_loop(0, lax.div(plan[COUNT] + (UNROLL - 1), UNROLL), body, 0)


def products(plan, blocks, tiles, n_out):
    width = blocks[0].shape[1]
    smem = pl.BlockSpec(memory_space=pltpu.SMEM)
    vmem = pl.BlockSpec(memory_space=pltpu.VMEM)
    return pl.pallas_call(
        products_kernel,
        out_shape=jax.ShapeDtypeStruct(((n_out + 1) * BLK, width), jnp.float32),
        in_specs=[smem] + [vmem] * len(blocks) + [vmem],
        out_specs=vmem,
        scratch_shapes=[pltpu.VMEM((len(blocks), 3 * BLK, width), jnp.bfloat16)],
        compiler_params=pltpu.CompilerParams(vmem_limit_bytes=16 * 2**20),
        cost_estimate=pl.CostEstimate(
            flops=32 * 3 * 2 * BLK * BLK * width, bytes_accessed=8 * 2**20, transcendentals=0
        ),
    )(plan, *blocks, tiles)


def shift(value, axis, by):
    n = lax.axis_size(axis)
    return lax.ppermute(value, axis, [(i, (i + by) % n) for i in range(n)])


def ring_hop(found, hop):
    n = lax.axis_size("bal")
    found[hop] = shift(found[hop - 1], "bal", 1)
    if n - hop > hop:
        found[n - hop] = shift(found[(n - hop + 1) % n], "bal", -1)


def ring_gather(value):
    found = {0: value}
    for hop in range(1, HOPS + 1):
        ring_hop(found, hop)
    return [found[h] for h in range(RING)]


def spread(value, axes):
    return lax.all_to_all(value, axes, split_axis=0, concat_axis=0, tiled=True)


def summed_everywhere(term):
    rows, width = term.shape
    half = rows // 2
    core = lax.axis_index("core")
    mine = lax.dynamic_slice_in_dim(term, core * half, half, 0)
    other = lax.dynamic_slice_in_dim(term, (1 - core) * half, half, 0)
    mine = mine + shift(other, "core", 1)
    chips = ("y", "x", "bal")
    n = lax.axis_size(chips)
    row = spread(mine, chips).reshape(n, half // n, width).sum(0)
    back = jnp.broadcast_to(row[None], (n, half // n, width)).reshape(half, width)
    mine = spread(back, chips)
    other = shift(mine, "core", 1)
    first = jnp.where(core == 0, mine, other)
    second = jnp.where(core == 0, other, mine)
    return jnp.concatenate([first, second], axis=0)


def over_the_links(
    grad_out, deriv_mask, weight, zcache, tile_values, tile_source, tile_slot, recv_target
):
    rows, width = grad_out.shape
    per_group = lax.axis_size("bal")
    slots = recv_target.shape[0]
    selector = (recv_target[:, None] == jnp.arange(per_group, dtype=jnp.int32)[None, :]).astype(
        jnp.float32
    )
    mask_float = deriv_mask.astype(jnp.float32)
    fixed_grad = grad_out
    for step in range(STEPS):
        group_rows = lax.all_gather(fixed_grad, "bal", axis=0, tiled=True)
        blocks = group_rows.reshape(per_group, BLK, width)
        partial_value = jnp.einsum(
            "tij,tjf->tif", tile_values, blocks[tile_source], precision=HIGHEST
        )
        outgoing = jnp.zeros((slots, BLK, width), jnp.float32).at[tile_slot].set(partial_value)
        incoming = spread(outgoing, GRP)
        sums = jnp.einsum("st,sif->tif", selector, incoming, precision=HIGHEST)
        owned = lax.psum_scatter(sums, "bal", scatter_dimension=0, tiled=True).reshape(rows, width)
        product = jnp.dot(owned, weight, precision=HIGHEST, preferred_element_type=jnp.float32)
        fixed_grad = mask_float * product + grad_out
    local_term = jnp.dot(
        fixed_grad.T, zcache, precision=HIGHEST, preferred_element_type=jnp.float32
    )
    return (lax.psum(local_term, ALL), fixed_grad)


def per_device(
    grad_out, deriv_mask, weight, zcache, tile_values, tile_source, tile_slot, recv_target
):
    rows, width = grad_out.shape
    n_bal = lax.axis_size("bal")
    chips = lax.axis_size(PLANE)
    bal = lax.axis_index("bal")
    core = lax.axis_index("core")
    per = tile_slot.shape[0]

    n_grp = lax.axis_size(GRP)
    asked = jnp.pad(recv_target.reshape(n_grp, -1), ((0, 0), (0, 126)))
    facts, ahead, behind = pack(bal, spread(asked, GRP), tile_slot, tile_source, tile_values)

    def hop(piece, size=None):
        part = slice(None) if size is None else slice(size * BLK)
        return [shift(piece[0][part], "bal", 1), shift(piece[1][part], "bal", -1)]

    blocks = {0: grad_out}
    long, middle, short = zip(ahead, behind)
    long1, middle1, short1 = hop(long), hop(middle), hop(short)
    ring_hop(blocks, 1)
    long1, middle1, short1, blocks, facts = lax.optimization_barrier(
        (long1, middle1, short1, blocks, facts)
    )
    long2, middle2 = hop(long1), hop(middle1)
    ring_hop(blocks, 2)
    facts = spread(jnp.broadcast_to(facts[None], (n_bal,) + facts.shape), "bal")
    long2, middle2, blocks, facts = lax.optimization_barrier((long2, middle2, blocks, facts))
    long3 = hop(long2)
    ring_hop(blocks, 3)
    plan = make_list(chips, per, jnp.stack([bal, core]), facts.reshape(n_bal * FACTS, BLK))
    long3, blocks, plan = lax.optimization_barrier((long3, blocks, plan))
    long4 = hop(long3, CAPS[3])
    ring_hop(blocks, 4)
    blocks = [blocks[h] for h in range(RING)]
    arrived = [[long1, middle1, short1], [long2, middle2], [long3], [long4]]
    buffers = [tile_values.reshape(per * BLK, BLK)]
    for _, hops, side in routes():
        buffers += [piece[side] for piece in arrived[hops - 1]]
    tiles = collect(plan, buffers)

    mask_float = deriv_mask.astype(jnp.float32)
    fixed_grad = grad_out
    half = chips * rows
    for step in range(STEPS):
        if step:
            blocks = ring_gather(fixed_grad)
        sums = products(plan, blocks, tiles, 2 * chips)
        partial_sum = sums[:half] + shift(sums[half : 2 * half], "core", 1)
        owned = spread(partial_sum, PLANE).reshape(chips, rows, width).sum(0)
        product = jnp.dot(owned, weight, precision=HIGHEST, preferred_element_type=jnp.float32)
        fixed_grad = mask_float * product + grad_out
    local_term = jnp.dot(
        fixed_grad.T, zcache, precision=HIGHEST, preferred_element_type=jnp.float32
    )
    weight_grad = summed_everywhere(jnp.where(plan[TOO_MANY] > 0, jnp.nan, local_term))
    return lax.cond(
        jnp.isnan(weight_grad[0, 0]),
        over_the_links,
        lambda *arguments: (weight_grad, fixed_grad),
        grad_out, deriv_mask, weight, zcache, tile_values, tile_source, tile_slot, recv_target,
    )


def solution(mesh):
    fine = Mesh(mesh.devices.reshape(4, 4, 2, mesh.shape["bal"]), ALL)
    in_specs = (
        P(ALL, None),
        P(ALL, None),
        P(),
        P(ALL, None),
        P(ALL, None, None),
        P(ALL),
        P(ALL),
        P(ALL),
    )
    out_specs = (P(), P(ALL, None))
    return jax.shard_map(
        per_device, mesh=fine, in_specs=in_specs, out_specs=out_specs, check_vma=False
    )
```

```python
import functools

import jax
import jax.numpy as jnp
from jax import lax
from jax.experimental import pallas as pl
from jax.experimental.pallas import tpu as pltpu
from jax.sharding import Mesh
from jax.sharding import PartitionSpec as P

STEPS = 3
BLK = 128
UNROLL = 4
RING, HOPS, FACTS = 8, 4, 8
CAPS = (22, 16, 7)
HELD = 64
PLANE = ("y", "x")
GRP = ("y", "x", "core")
ALL = ("y", "x", "core", "bal")
HIGHEST = lax.Precision.HIGHEST


def split(value):
    high = value.astype(jnp.bfloat16)
    low = (value - high.astype(jnp.float32)).astype(jnp.bfloat16)
    return high, low


def facts_kernel(tgt, tile_slot, tile_source, facts):
    def one(j, carry):
        s = tile_slot[j]
        facts[0, j] = s >> 1
        facts[1, j] = tgt[s >> 1, s & 1]
        facts[2, j] = tile_source[j]
        return carry

    lax.fori_loop(0, tile_slot.shape[0], one, 0)


def make_facts(tgt, tile_slot, tile_source):
    smem = pl.BlockSpec(memory_space=pltpu.SMEM)
    return pl.pallas_call(
        facts_kernel,
        out_shape=jax.ShapeDtypeStruct((FACTS, BLK), jnp.int32),
        in_specs=[smem] * 3,
        out_specs=smem,
    )(tgt, tile_slot, tile_source)


def pack_kernel(plan, ahead, behind, *refs):
    outs, sems = refs[:-1], refs[-1]
    copies = []
    for side, (tiles, out) in enumerate(zip((ahead, behind), outs)):
        for k in range(CAPS[0]):
            copies.append(
                pltpu.make_async_copy(
                    tiles.at[plan[ORDER[side] + k]], out.at[k], sems.at[side * CAPS[0] + k]
                )
            )
    for copy in copies:
        copy.start()
    for copy in copies:
        copy.wait()


def pack(plan, ahead, behind):
    vmem = pl.BlockSpec(memory_space=pltpu.VMEM)
    out = jax.ShapeDtypeStruct((CAPS[0],) + ahead.shape[1:], jnp.float32)
    return pl.pallas_call(
        pack_kernel,
        out_shape=(out, out),
        in_specs=[pl.BlockSpec(memory_space=pltpu.SMEM)] + [pl.BlockSpec(memory_space=pl.ANY)] * 2,
        out_specs=(vmem, vmem),
        scratch_shapes=[pltpu.SemaphoreType.DMA((2 * CAPS[0],))],
        compiler_params=pltpu.CompilerParams(vmem_limit_bytes=8 * 2**20),
    )(plan, ahead, behind)


SOURCE, TARGET, OWN, ENDS, FIRST = 0, HELD + 1, 2 * (HELD + 1), 3 * (HELD + 1), 4 * (HELD + 1)
COUNT, TOO_MANY, ORDER = 5 * (HELD + 1), 5 * (HELD + 1) + 1, (6 * (HELD + 1), 7 * (HELD + 1))
LISTED = 8 * (HELD + 1)


def routes():
    return [(h if side == 0 else RING - h, h, side) for h in range(1, HOPS + 1) for side in (0, 1)]


def list_kernel(chips, per, here, facts, plan):
    bal, core = here[0], here[1]
    def clear(k, carry):
        plan[SOURCE + k] = 0
        return carry

    lax.fori_loop(0, HELD + 1, clear, 0)

    def sender(row):
        return ((bal - row + RING) & (RING - 1)) * FACTS

    def note(k, row, j):
        at = jnp.minimum(k, HELD)
        group = facts[sender(row), j]
        plan[SOURCE + at] = (bal - facts[sender(row) + 2, j] + RING) & (RING - 1)
        plan[TARGET + at] = (group >> 1) + chips * ((group & 1) ^ core)
        plan[OWN + at] = j

    def way(row, j):
        return (facts[sender(row) + 1, j] - bal + row + RING) & (RING - 1)

    def own(j, k):
        note(k, 0, j)
        return k + (way(0, j) == 0).astype(jnp.int32)

    total = lax.fori_loop(0, per, own, jnp.int32(0))
    plan[ENDS] = jnp.minimum(total, HELD)
    plan[FIRST] = 0
    too_many = jnp.int32(0)
    index = 1
    for row, hops, side in routes():

        def one(j, carry, row=row, hops=hops, side=side):
            k, farther, opposite = carry
            d = way(row, j)
            note(k, row, j)
            is_opposite = d == HOPS
            if hops == HOPS:
                mine = is_opposite & ((opposite & 1) == side)
                far = jnp.int32(0)
            else:
                mine = d == row
                if side == 0:
                    far = ((d > row) & (d < HOPS)).astype(jnp.int32)
                else:
                    far = ((d < row) & (d > HOPS)).astype(jnp.int32)
            return (
                k + mine.astype(jnp.int32),
                farther + far,
                opposite + is_opposite.astype(jnp.int32),
            )

        stop, farther, opposite = lax.fori_loop(
            0, per, one, (total, jnp.int32(0), jnp.int32(0))
        )
        if hops > 1:
            if hops < HOPS:
                farther = farther + ((opposite + 1 - side) >> 1)
            first, last, limit = farther, farther + stop - total, CAPS[hops - 2]
            too_many = jnp.where(last > limit, 1, too_many)
            stop = total + jnp.minimum(last, limit) - jnp.minimum(first, limit)
            plan[FIRST + index] = first
        total = stop
        plan[ENDS + index] = jnp.minimum(total, HELD)
        index += 1
    plan[COUNT] = jnp.minimum(total, HELD)
    plan[TOO_MANY] = jnp.where(total > HELD, 1, too_many)

    def pad(k, carry):
        plan[TARGET + k] = 2 * chips
        return carry

    lax.fori_loop(jnp.minimum(total, HELD), HELD + 1, pad, 0)

    for side in range(2):
        row = 1 if side == 0 else RING - 1

        def hops_of(j, turn, side=side, row=row):
            d = (facts[sender(row) + 1, j] - bal + row + 2 * RING) & (RING - 1)
            is_opposite = d == HOPS
            ahead = jnp.where(is_opposite, jnp.where(turn == 0, HOPS, 0), jnp.where(d < HOPS, d, 0))
            behind = jnp.where(
                is_opposite, jnp.where(turn == 1, HOPS, 0), jnp.where(d > HOPS, RING - d, 0)
            )
            return (behind if side else ahead), turn ^ is_opposite.astype(jnp.int32)

        def count(j, carry, hops_of=hops_of):
            four, three, turn = carry
            hops, turn = hops_of(j, turn)
            return four + (hops == 4).astype(jnp.int32), three + (hops == 3).astype(jnp.int32), turn

        zero = jnp.int32(0)
        four, three, _ = lax.fori_loop(0, per, count, (zero, zero, zero))

        def clear_order(k, carry, side=side):
            plan[ORDER[side] + k] = 0
            return carry

        lax.fori_loop(0, per, clear_order, 0)

        def place(j, carry, side=side, hops_of=hops_of):
            at4, at3, at2, turn = carry
            hops, turn = hops_of(j, turn)
            where = jnp.where(
                hops == 4, at4, jnp.where(hops == 3, at3, jnp.where(hops == 2, at2, per))
            )
            plan[ORDER[side] + where] = j
            return (
                at4 + (hops == 4).astype(jnp.int32),
                at3 + (hops == 3).astype(jnp.int32),
                at2 + (hops == 2).astype(jnp.int32),
                turn,
            )

        lax.fori_loop(0, per, place, (zero, four, four + three, zero))


def make_list(chips, per, here, facts):
    smem = pl.BlockSpec(memory_space=pltpu.SMEM)
    return pl.pallas_call(
        functools.partial(list_kernel, chips, per),
        out_shape=jax.ShapeDtypeStruct((LISTED,), jnp.int32),
        in_specs=[smem, smem],
        out_specs=smem,
    )(here, facts)


def collect_kernel(begun, plan, *refs):
    buffers, (out, held, sems) = refs[: -3 - (begun > 0)], refs[-3:]

    def copy(buffer, k, where):
        return pltpu.make_async_copy(buffer.at[where], held.at[k], sems.at[k])

    def start_of(i):
        return plan[ENDS + i - 1] if i else 0

    for i, buffer in enumerate(buffers, begun):
        start = start_of(i)

        def begin(k, carry, i=i, buffer=buffer, start=start):
            copy(buffer, k, plan[OWN + k] if i < 3 else plan[FIRST + i] + k - start).start()
            return carry

        lax.fori_loop(start, plan[ENDS + i], begin, 0)

    def finish(k, carry):
        copy(buffers[0], k, 0).wait()
        high, low = split(held[k])
        out[k] = jnp.concatenate([high, low], axis=1)
        return carry

    lax.fori_loop(start_of(begun), plan[ENDS + begun + len(buffers) - 1], finish, 0)


def collect(plan, begun, buffers, tiles=None):
    smem = pl.BlockSpec(memory_space=pltpu.SMEM)
    vmem = pl.BlockSpec(memory_space=pltpu.VMEM)
    operands = [plan] + list(buffers) + ([] if tiles is None else [tiles])
    return pl.pallas_call(
        functools.partial(collect_kernel, begun),
        out_shape=jax.ShapeDtypeStruct((HELD, BLK, 2 * BLK), jnp.bfloat16),
        in_specs=[smem]
        + [pl.BlockSpec(memory_space=pl.ANY)] * len(buffers)
        + ([] if tiles is None else [vmem]),
        out_specs=vmem,
        input_output_aliases={} if tiles is None else {len(operands) - 1: 0},
        scratch_shapes=[
            pltpu.VMEM((HELD, BLK, BLK), jnp.float32),
            pltpu.SemaphoreType.DMA((HELD,)),
        ],
        compiler_params=pltpu.CompilerParams(vmem_limit_bytes=16 * 2**20),
    )(*operands)


def products_kernel(plan, *refs):
    n_blocks = len(refs) - 3
    blocks = refs[:n_blocks]
    tiles, out, rhs = refs[n_blocks:]
    for i, block in enumerate(blocks):
        high, low = split(block[0:BLK])
        rhs[i, 0:BLK] = high
        rhs[i, BLK : 2 * BLK] = high
        rhs[i, 2 * BLK : 3 * BLK] = low
    out[...] = jnp.zeros_like(out)

    def body(turn, carry):
        first = turn * UNROLL
        found = []
        for k in range(UNROLL):
            tile = tiles[first + k]
            lhs = jnp.concatenate([tile, tile[:, :BLK]], axis=1)
            found.append(
                jnp.dot(lhs, rhs[plan[SOURCE + first + k]], preferred_element_type=jnp.float32)
            )
        for k in range(UNROLL):
            rows = pl.ds(pl.multiple_of(plan[TARGET + first + k] * BLK, BLK), BLK)
            out[rows] += found[k]
        return carry

    lax.fori_loop(0, lax.div(plan[COUNT] + (UNROLL - 1), UNROLL), body, 0)


def products(plan, blocks, tiles, n_out):
    width = blocks[0].shape[1]
    smem = pl.BlockSpec(memory_space=pltpu.SMEM)
    vmem = pl.BlockSpec(memory_space=pltpu.VMEM)
    return pl.pallas_call(
        products_kernel,
        out_shape=jax.ShapeDtypeStruct(((n_out + 1) * BLK, width), jnp.float32),
        in_specs=[smem] + [vmem] * len(blocks) + [vmem],
        out_specs=vmem,
        scratch_shapes=[pltpu.VMEM((len(blocks), 3 * BLK, width), jnp.bfloat16)],
        compiler_params=pltpu.CompilerParams(vmem_limit_bytes=16 * 2**20),
        cost_estimate=pl.CostEstimate(
            flops=32 * 3 * 2 * BLK * BLK * width, bytes_accessed=8 * 2**20, transcendentals=0
        ),
    )(plan, *blocks, tiles)


def shift(value, axis, by):
    n = lax.axis_size(axis)
    return lax.ppermute(value, axis, [(i, (i + by) % n) for i in range(n)])


def ring_hop(found, hop):
    n = lax.axis_size("bal")
    found[hop] = shift(found[hop - 1], "bal", 1)
    if n - hop > hop:
        found[n - hop] = shift(found[(n - hop + 1) % n], "bal", -1)


def ring_gather(value):
    found = {0: value}
    for hop in range(1, HOPS + 1):
        ring_hop(found, hop)
    return [found[h] for h in range(RING)]


def spread(value, axes):
    return lax.all_to_all(value, axes, split_axis=0, concat_axis=0, tiled=True)


def summed_everywhere(term):
    rows, width = term.shape
    half = rows // 2
    core = lax.axis_index("core")
    mine = lax.dynamic_slice_in_dim(term, core * half, half, 0)
    other = lax.dynamic_slice_in_dim(term, (1 - core) * half, half, 0)
    mine = mine + shift(other, "core", 1)
    chips = ("y", "x", "bal")
    n = lax.axis_size(chips)
    row = spread(mine, chips).reshape(n, half // n, width).sum(0)
    back = jnp.broadcast_to(row[None], (n, half // n, width)).reshape(half, width)
    mine = spread(back, chips)
    other = shift(mine, "core", 1)
    first = jnp.where(core == 0, mine, other)
    second = jnp.where(core == 0, other, mine)
    return jnp.concatenate([first, second], axis=0)


def over_the_links(
    grad_out, deriv_mask, weight, zcache, tile_values, tile_source, tile_slot, recv_target
):
    rows, width = grad_out.shape
    per_group = lax.axis_size("bal")
    slots = recv_target.shape[0]
    selector = (recv_target[:, None] == jnp.arange(per_group, dtype=jnp.int32)[None, :]).astype(
        jnp.float32
    )
    mask_float = deriv_mask.astype(jnp.float32)
    fixed_grad = grad_out
    for step in range(STEPS):
        group_rows = lax.all_gather(fixed_grad, "bal", axis=0, tiled=True)
        blocks = group_rows.reshape(per_group, BLK, width)
        partial_value = jnp.einsum(
            "tij,tjf->tif", tile_values, blocks[tile_source], precision=HIGHEST
        )
        outgoing = jnp.zeros((slots, BLK, width), jnp.float32).at[tile_slot].set(partial_value)
        incoming = spread(outgoing, GRP)
        sums = jnp.einsum("st,sif->tif", selector, incoming, precision=HIGHEST)
        owned = lax.psum_scatter(sums, "bal", scatter_dimension=0, tiled=True).reshape(rows, width)
        product = jnp.dot(owned, weight, precision=HIGHEST, preferred_element_type=jnp.float32)
        fixed_grad = mask_float * product + grad_out
    local_term = jnp.dot(
        fixed_grad.T, zcache, precision=HIGHEST, preferred_element_type=jnp.float32
    )
    return (lax.psum(local_term, ALL), fixed_grad)


def per_device(
    grad_out, deriv_mask, weight, zcache, tile_values, tile_source, tile_slot, recv_target
):
    rows, width = grad_out.shape
    n_bal = lax.axis_size("bal")
    chips = lax.axis_size(PLANE)
    bal = lax.axis_index("bal")
    core = lax.axis_index("core")
    per = tile_slot.shape[0]

    def hop(pair, size=None):
        part = slice(None) if size is None else slice(size)
        return [shift(pair[0][part], "bal", 1), shift(pair[1][part], "bal", -1)]

    blocks = {0: grad_out}
    came1 = hop([tile_values, tile_values])
    ring_hop(blocks, 1)
    n_grp = lax.axis_size(GRP)
    asked = jnp.pad(recv_target.reshape(n_grp, -1), ((0, 0), (0, 126)))
    facts = make_facts(spread(asked, GRP), tile_slot, tile_source)
    facts = spread(jnp.broadcast_to(facts[None], (n_bal,) + facts.shape), "bal")
    plan = make_list(chips, per, jnp.stack([bal, core]), facts.reshape(n_bal * FACTS, BLK))
    came1, blocks, plan = lax.optimization_barrier((came1, blocks, plan))
    came2 = hop(pack(plan, *came1))
    ring_hop(blocks, 2)
    tiles = collect(plan, 0, [tile_values] + came1)
    came2, blocks, tiles = lax.optimization_barrier((came2, blocks, tiles))
    came3 = hop(came2, CAPS[1])
    ring_hop(blocks, 3)
    tiles = collect(plan, 3, came2, tiles)
    came3, blocks, tiles = lax.optimization_barrier((came3, blocks, tiles))
    came4 = hop(came3, CAPS[2])
    ring_hop(blocks, 4)
    tiles = collect(plan, 5, came3, tiles)
    tiles = collect(plan, 7, came4, tiles)
    blocks = [blocks[h] for h in range(RING)]

    mask_float = deriv_mask.astype(jnp.float32)
    fixed_grad = grad_out
    half = chips * rows
    for step in range(STEPS):
        if step:
            blocks = ring_gather(fixed_grad)
        sums = products(plan, blocks, tiles, 2 * chips)
        partial_sum = sums[:half] + shift(sums[half : 2 * half], "core", 1)
        owned = spread(partial_sum, PLANE).reshape(chips, rows, width).sum(0)
        product = jnp.dot(owned, weight, precision=HIGHEST, preferred_element_type=jnp.float32)
        fixed_grad = mask_float * product + grad_out
    local_term = jnp.dot(
        fixed_grad.T, zcache, precision=HIGHEST, preferred_element_type=jnp.float32
    )
    weight_grad = summed_everywhere(jnp.where(plan[TOO_MANY] > 0, jnp.nan, local_term))
    return lax.cond(
        jnp.isnan(weight_grad[0, 0]),
        over_the_links,
        lambda *arguments: (weight_grad, fixed_grad),
        grad_out, deriv_mask, weight, zcache, tile_values, tile_source, tile_slot, recv_target,
    )


def solution(mesh):
    fine = Mesh(mesh.devices.reshape(4, 4, 2, mesh.shape["bal"]), ALL)
    in_specs = (
        P(ALL, None),
        P(ALL, None),
        P(),
        P(ALL, None),
        P(ALL, None, None),
        P(ALL),
        P(ALL),
        P(ALL),
    )
    out_specs = (P(), P(ALL, None))
    return jax.shard_map(
        per_device, mesh=fine, in_specs=in_specs, out_specs=out_specs, check_vma=False
    )
```

```python
import functools

import jax
import jax.numpy as jnp
from jax import lax
from jax.experimental import pallas as pl
from jax.experimental.pallas import tpu as pltpu
from jax.sharding import Mesh
from jax.sharding import PartitionSpec as P

STEPS = 3
BLK = 128
UNROLL = 8
RING, HOPS = 8, 4
CAPS = (22, 16, 7)
HELD = 64
PLANE = ("y", "x")
GRP = ("y", "x", "core")
ALL = ("y", "x", "core", "bal")
HIGHEST = lax.Precision.HIGHEST


def split(value):
    high = value.astype(jnp.bfloat16)
    low = (value - high.astype(jnp.float32)).astype(jnp.bfloat16)
    return high, low


def pack_kernel(plan, ahead, behind, *refs):
    outs, sems = refs[:-1], refs[-1]
    copies = []
    for side, (tiles, out) in enumerate(zip((ahead, behind), outs)):
        for k in range(CAPS[0]):
            copies.append(
                pltpu.make_async_copy(
                    tiles.at[plan[ORDER[side] + k]], out.at[k], sems.at[side * CAPS[0] + k]
                )
            )
    for copy in copies:
        copy.start()
    for copy in copies:
        copy.wait()


def pack(plan, ahead, behind):
    vmem = pl.BlockSpec(memory_space=pltpu.VMEM)
    out = jax.ShapeDtypeStruct((CAPS[0],) + ahead.shape[1:], jnp.float32)
    return pl.pallas_call(
        pack_kernel,
        out_shape=(out, out),
        in_specs=[pl.BlockSpec(memory_space=pltpu.SMEM)] + [pl.BlockSpec(memory_space=pl.ANY)] * 2,
        out_specs=(vmem, vmem),
        scratch_shapes=[pltpu.SemaphoreType.DMA((2 * CAPS[0],))],
        compiler_params=pltpu.CompilerParams(vmem_limit_bytes=4 * 2**20),
    )(plan, ahead, behind)


SOURCE, TARGET, OWN, ENDS, FIRST = 0, HELD + 1, 2 * (HELD + 1), 3 * (HELD + 1), 4 * (HELD + 1)
COUNT, TOO_MANY, ORDER = 5 * (HELD + 1), 5 * (HELD + 1) + 1, (6 * (HELD + 1), 7 * (HELD + 1))
LISTED = 8 * (HELD + 1)


def routes():
    return [(h if side == 0 else RING - h, h, side) for h in range(1, HOPS + 1) for side in (0, 1)]


def list_kernel(chips, per, here, held, asked, plan, wanted):
    bal, core = here[0], here[1]
    slots, sources = held.shape[1] - 2 * per, held.shape[1] - per
    for device in range(RING):

        def look(j, carry, device=device):
            s = held[device, slots + j]
            wanted[device, j] = asked[s >> 1, 2 * device + (s & 1)]
            return carry

        lax.fori_loop(0, per, look, 0, unroll=8)

    def clear(k, carry):
        plan[SOURCE + k] = 0
        return carry

    lax.fori_loop(0, HELD + 1, clear, 0)

    def sender(row):
        return (bal - row + RING) & (RING - 1)

    def note(k, row, j):
        at = jnp.minimum(k, HELD)
        group = held[sender(row), slots + j] >> 1
        plan[SOURCE + at] = (bal - held[sender(row), sources + j] + RING) & (RING - 1)
        plan[TARGET + at] = (group >> 1) + chips * ((group & 1) ^ core)
        plan[OWN + at] = j

    def way(row, j):
        return (wanted[sender(row), j] - bal + row + RING) & (RING - 1)

    def own(j, k):
        note(k, 0, j)
        return k + (way(0, j) == 0).astype(jnp.int32)

    total = lax.fori_loop(0, per, own, jnp.int32(0), unroll=8)
    plan[ENDS] = jnp.minimum(total, HELD)
    plan[FIRST] = 0
    too_many = jnp.int32(0)
    index = 1
    for row, hops, side in routes():

        def one(j, carry, row=row, hops=hops, side=side):
            k, farther, opposite = carry
            d = way(row, j)
            note(k, row, j)
            is_opposite = d == HOPS
            if hops == HOPS:
                mine = is_opposite & ((opposite & 1) == side)
                far = jnp.int32(0)
            else:
                mine = d == row
                if side == 0:
                    far = ((d > row) & (d < HOPS)).astype(jnp.int32)
                else:
                    far = ((d < row) & (d > HOPS)).astype(jnp.int32)
            return (
                k + mine.astype(jnp.int32),
                farther + far,
                opposite + is_opposite.astype(jnp.int32),
            )

        stop, farther, opposite = lax.fori_loop(
            0, per, one, (total, jnp.int32(0), jnp.int32(0)), unroll=8
        )
        if hops > 1:
            if hops < HOPS:
                farther = farther + ((opposite + 1 - side) >> 1)
            first, last, limit = farther, farther + stop - total, CAPS[hops - 2]
            too_many = jnp.where(last > limit, 1, too_many)
            stop = total + jnp.minimum(last, limit) - jnp.minimum(first, limit)
            plan[FIRST + index] = first
        total = stop
        plan[ENDS + index] = jnp.minimum(total, HELD)
        index += 1
    plan[COUNT] = jnp.minimum(total, HELD)
    plan[TOO_MANY] = jnp.where(total > HELD, 1, too_many)

    def pad(k, carry):
        plan[TARGET + k] = 2 * chips
        return carry

    lax.fori_loop(jnp.minimum(total, HELD), HELD + 1, pad, 0)

    for side in range(2):
        row = 1 if side == 0 else RING - 1

        def hops_of(j, turn, side=side, row=row):
            d = way(row, j)
            is_opposite = d == HOPS
            ahead = jnp.where(is_opposite, jnp.where(turn == 0, HOPS, 0), jnp.where(d < HOPS, d, 0))
            behind = jnp.where(
                is_opposite, jnp.where(turn == 1, HOPS, 0), jnp.where(d > HOPS, RING - d, 0)
            )
            return (behind if side else ahead), turn ^ is_opposite.astype(jnp.int32)

        def count(j, carry, hops_of=hops_of):
            four, three, turn = carry
            hops, turn = hops_of(j, turn)
            return four + (hops == 4).astype(jnp.int32), three + (hops == 3).astype(jnp.int32), turn

        zero = jnp.int32(0)
        four, three, _ = lax.fori_loop(0, per, count, (zero, zero, zero), unroll=8)

        def clear_order(k, carry, side=side):
            plan[ORDER[side] + k] = 0
            return carry

        lax.fori_loop(0, per, clear_order, 0, unroll=8)

        def place(j, carry, side=side, hops_of=hops_of):
            at4, at3, at2, turn = carry
            hops, turn = hops_of(j, turn)
            where = jnp.where(
                hops == 4, at4, jnp.where(hops == 3, at3, jnp.where(hops == 2, at2, per))
            )
            plan[ORDER[side] + where] = j
            return (
                at4 + (hops == 4).astype(jnp.int32),
                at3 + (hops == 3).astype(jnp.int32),
                at2 + (hops == 2).astype(jnp.int32),
                turn,
            )

        lax.fori_loop(0, per, place, (zero, four, four + three, zero), unroll=8)


def make_list(chips, per, here, held, asked):
    smem = pl.BlockSpec(memory_space=pltpu.SMEM)
    return pl.pallas_call(
        functools.partial(list_kernel, chips, per),
        out_shape=jax.ShapeDtypeStruct((LISTED,), jnp.int32),
        in_specs=[smem] * 3,
        out_specs=smem,
        scratch_shapes=[pltpu.SMEM((RING, per), jnp.int32)],
    )(here, held, asked)


def collect_kernel(begun, plan, *refs):
    buffers, (out, held, sems) = refs[: -3 - (begun > 0)], refs[-3:]

    def copy(buffer, k, where):
        return pltpu.make_async_copy(buffer.at[where], held.at[k], sems.at[k])

    def start_of(i):
        return plan[ENDS + i - 1] if i else 0

    for i, buffer in enumerate(buffers, begun):
        start = start_of(i)

        def begin(k, carry, i=i, buffer=buffer, start=start):
            copy(buffer, k, plan[OWN + k] if i < 3 else plan[FIRST + i] + k - start).start()
            return carry

        lax.fori_loop(start, plan[ENDS + i], begin, 0)

    def finish(k, carry):
        copy(buffers[0], k, 0).wait()
        high, low = split(held[k])
        out[k] = jnp.concatenate([high, low], axis=1)
        return carry

    lax.fori_loop(start_of(begun), plan[ENDS + begun + len(buffers) - 1], finish, 0)


def collect(plan, begun, buffers, tiles=None):
    smem = pl.BlockSpec(memory_space=pltpu.SMEM)
    vmem = pl.BlockSpec(memory_space=pltpu.VMEM)
    operands = [plan] + list(buffers) + ([] if tiles is None else [tiles])
    return pl.pallas_call(
        functools.partial(collect_kernel, begun),
        out_shape=jax.ShapeDtypeStruct((HELD, BLK, 2 * BLK), jnp.bfloat16),
        in_specs=[smem]
        + [pl.BlockSpec(memory_space=pl.ANY)] * len(buffers)
        + ([] if tiles is None else [vmem]),
        out_specs=vmem,
        input_output_aliases={} if tiles is None else {len(operands) - 1: 0},
        scratch_shapes=[
            pltpu.VMEM((HELD, BLK, BLK), jnp.float32),
            pltpu.SemaphoreType.DMA((HELD,)),
        ],
        compiler_params=pltpu.CompilerParams(vmem_limit_bytes=6 * 2**20),
    )(*operands)


def products_kernel(plan, *refs):
    n_blocks = len(refs) - 3
    blocks = refs[:n_blocks]
    tiles, out, rhs = refs[n_blocks:]
    for i, block in enumerate(blocks):
        high, low = split(block[0:BLK])
        rhs[i, 0:BLK] = high
        rhs[i, BLK : 2 * BLK] = high
        rhs[i, 2 * BLK : 3 * BLK] = low
    out[...] = jnp.zeros_like(out)

    def body(turn, carry):
        first = turn * UNROLL
        found = []
        for k in range(UNROLL):
            tile = tiles[first + k]
            lhs = jnp.concatenate([tile, tile[:, :BLK]], axis=1)
            found.append(
                jnp.dot(lhs, rhs[plan[SOURCE + first + k]], preferred_element_type=jnp.float32)
            )
        for k in range(UNROLL):
            rows = pl.ds(pl.multiple_of(plan[TARGET + first + k] * BLK, BLK), BLK)
            out[rows] += found[k]
        return carry

    lax.fori_loop(0, lax.div(plan[COUNT] + (UNROLL - 1), UNROLL), body, 0)


def products(plan, blocks, tiles, n_out):
    width = blocks[0].shape[1]
    smem = pl.BlockSpec(memory_space=pltpu.SMEM)
    vmem = pl.BlockSpec(memory_space=pltpu.VMEM)
    return pl.pallas_call(
        products_kernel,
        out_shape=jax.ShapeDtypeStruct(((n_out + 1) * BLK, width), jnp.float32),
        in_specs=[smem] + [vmem] * len(blocks) + [vmem],
        out_specs=vmem,
        scratch_shapes=[pltpu.VMEM((len(blocks), 3 * BLK, width), jnp.bfloat16)],
        compiler_params=pltpu.CompilerParams(vmem_limit_bytes=6 * 2**20),
        cost_estimate=pl.CostEstimate(
            flops=32 * 3 * 2 * BLK * BLK * width, bytes_accessed=8 * 2**20, transcendentals=0
        ),
    )(plan, *blocks, tiles)


def shift(value, axis, by):
    n = lax.axis_size(axis)
    return lax.ppermute(value, axis, [(i, (i + by) % n) for i in range(n)])


def ring_hop(found, hop):
    n = lax.axis_size("bal")
    found[hop] = shift(found[hop - 1], "bal", 1)
    if n - hop > hop:
        found[n - hop] = shift(found[(n - hop + 1) % n], "bal", -1)


def ring_gather(value):
    found = {0: value}
    ring_hop(found, 1)
    found[HOPS] = shift(value, "bal", HOPS)
    for hop in range(2, HOPS):
        ring_hop(found, hop)
    return [found[h] for h in range(RING)]


def spread(value, axes):
    return lax.all_to_all(value, axes, split_axis=0, concat_axis=0, tiled=True)


def summed_everywhere(term):
    rows, width = term.shape
    half = rows // 2
    core = lax.axis_index("core")
    mine = lax.dynamic_slice_in_dim(term, core * half, half, 0)
    other = lax.dynamic_slice_in_dim(term, (1 - core) * half, half, 0)
    mine = mine + shift(other, "core", 1)
    chips = ("y", "x", "bal")
    n = lax.axis_size(chips)
    row = spread(mine, chips).reshape(n, half // n, width).sum(0)
    back = jnp.broadcast_to(row[None], (n, half // n, width)).reshape(half, width)
    mine = spread(back, chips)
    other = shift(mine, "core", 1)
    first = jnp.where(core == 0, mine, other)
    second = jnp.where(core == 0, other, mine)
    return jnp.concatenate([first, second], axis=0)


def over_the_links(
    grad_out, deriv_mask, weight, zcache, tile_values, tile_source, tile_slot, recv_target
):
    rows, width = grad_out.shape
    per_group = lax.axis_size("bal")
    slots = recv_target.shape[0]
    selector = (recv_target[:, None] == jnp.arange(per_group, dtype=jnp.int32)[None, :]).astype(
        jnp.float32
    )
    mask_float = deriv_mask.astype(jnp.float32)
    fixed_grad = grad_out
    for step in range(STEPS):
        group_rows = lax.all_gather(fixed_grad, "bal", axis=0, tiled=True)
        blocks = group_rows.reshape(per_group, BLK, width)
        partial_value = jnp.einsum(
            "tij,tjf->tif", tile_values, blocks[tile_source], precision=HIGHEST
        )
        outgoing = jnp.zeros((slots, BLK, width), jnp.float32).at[tile_slot].set(partial_value)
        incoming = spread(outgoing, GRP)
        sums = jnp.einsum("st,sif->tif", selector, incoming, precision=HIGHEST)
        owned = lax.psum_scatter(sums, "bal", scatter_dimension=0, tiled=True).reshape(rows, width)
        product = jnp.dot(owned, weight, precision=HIGHEST, preferred_element_type=jnp.float32)
        fixed_grad = mask_float * product + grad_out
    local_term = jnp.dot(
        fixed_grad.T, zcache, precision=HIGHEST, preferred_element_type=jnp.float32
    )
    return (lax.psum(local_term, ALL), fixed_grad)


def per_device(
    grad_out, deriv_mask, weight, zcache, tile_values, tile_source, tile_slot, recv_target
):
    rows, width = grad_out.shape
    n_bal = lax.axis_size("bal")
    chips = lax.axis_size(PLANE)
    bal = lax.axis_index("bal")
    core = lax.axis_index("core")
    per = tile_slot.shape[0]

    def hop(pair, size=None):
        part = slice(None) if size is None else slice(size)
        return [shift(pair[0][part], "bal", 1), shift(pair[1][part], "bal", -1)]

    blocks = {0: grad_out}
    ring_hop(blocks, 1)
    held = jnp.concatenate([recv_target, tile_slot, tile_source])
    held = spread(jnp.broadcast_to(held[None], (n_bal,) + held.shape), "bal")
    tile_values, held = lax.optimization_barrier((tile_values, held))
    came1 = hop([tile_values, tile_values])
    slots = recv_target.shape[0]
    n_grp = lax.axis_size(GRP)
    asked = held[:, :slots].reshape(n_bal, n_grp, -1).transpose(1, 0, 2).reshape(n_grp, -1)
    asked = spread(jnp.pad(asked, ((0, 0), (0, BLK - asked.shape[1]))), GRP)
    plan = make_list(chips, per, jnp.stack([bal, core]), held, asked)
    came1, blocks, plan = lax.optimization_barrier((came1, blocks, plan))
    came2 = hop(pack(plan, *came1))
    ring_hop(blocks, 2)
    tiles = collect(plan, 0, [tile_values] + came1)
    came2, blocks, tiles = lax.optimization_barrier((came2, blocks, tiles))
    came3 = hop(came2, CAPS[1])
    ring_hop(blocks, 3)
    tiles = collect(plan, 3, came2, tiles)
    came3, blocks, tiles = lax.optimization_barrier((came3, blocks, tiles))
    came4 = hop(came3, CAPS[2])
    ring_hop(blocks, 4)
    tiles = collect(plan, 5, came3, tiles)
    tiles = collect(plan, 7, came4, tiles)
    blocks = [blocks[h] for h in range(RING)]

    mask_float = deriv_mask.astype(jnp.float32)
    fixed_grad = grad_out
    half = chips * rows
    for step in range(STEPS):
        if step:
            blocks = ring_gather(fixed_grad)
        sums = products(plan, blocks, tiles, 2 * chips)
        partial_sum = sums[:half] + shift(sums[half : 2 * half], "core", 1)
        owned = spread(partial_sum, PLANE).reshape(chips, rows, width).sum(0)
        product = jnp.dot(owned, weight, precision=HIGHEST, preferred_element_type=jnp.float32)
        fixed_grad = mask_float * product + grad_out
    local_term = jnp.dot(
        fixed_grad.T, zcache, precision=HIGHEST, preferred_element_type=jnp.float32
    )
    weight_grad = summed_everywhere(jnp.where(plan[TOO_MANY] > 0, jnp.nan, local_term))
    return lax.cond(
        jnp.isnan(weight_grad[0, 0]),
        over_the_links,
        lambda *arguments: (weight_grad, fixed_grad),
        grad_out, deriv_mask, weight, zcache, tile_values, tile_source, tile_slot, recv_target,
    )


def solution(mesh):
    fine = Mesh(mesh.devices.reshape(4, 4, 2, mesh.shape["bal"]), ALL)
    in_specs = (
        P(ALL, None),
        P(ALL, None),
        P(),
        P(ALL, None),
        P(ALL, None, None),
        P(ALL),
        P(ALL),
        P(ALL),
    )
    out_specs = (P(), P(ALL, None))
    return jax.shard_map(
        per_device, mesh=fine, in_specs=in_specs, out_specs=out_specs, check_vma=False
    )
```

```python
import functools

import jax
import jax.numpy as jnp
from jax import lax
from jax.experimental import pallas as pl
from jax.experimental.pallas import tpu as pltpu
from jax.sharding import Mesh
from jax.sharding import PartitionSpec as P

STEPS = 3
BLK = 128
UNROLL = 8
RING, HOPS = 8, 4
CAPS = (22, 16, 7)
HELD = 64
PLANE = ("y", "x")
GRP = ("y", "x", "core")
ALL = ("y", "x", "core", "bal")
HIGHEST = lax.Precision.HIGHEST


def split(value):
    high = value.astype(jnp.bfloat16)
    low = (value - high.astype(jnp.float32)).astype(jnp.bfloat16)
    return high, low


def pack_kernel(plan, ahead, behind, *refs):
    outs, sems = refs[:-1], refs[-1]
    copies = []
    for side, (tiles, out) in enumerate(zip((ahead, behind), outs)):
        for k in range(CAPS[0]):
            copies.append(
                pltpu.make_async_copy(
                    tiles.at[plan[ORDER[side] + k]], out.at[k], sems.at[side * CAPS[0] + k]
                )
            )
    for copy in copies:
        copy.start()
    for copy in copies:
        copy.wait()


def pack(plan, ahead, behind):
    vmem = pl.BlockSpec(memory_space=pltpu.VMEM)
    out = jax.ShapeDtypeStruct((CAPS[0],) + ahead.shape[1:], jnp.float32)
    return pl.pallas_call(
        pack_kernel,
        out_shape=(out, out),
        in_specs=[pl.BlockSpec(memory_space=pltpu.SMEM)] + [pl.BlockSpec(memory_space=pl.ANY)] * 2,
        out_specs=(vmem, vmem),
        scratch_shapes=[pltpu.SemaphoreType.DMA((2 * CAPS[0],))],
        compiler_params=pltpu.CompilerParams(vmem_limit_bytes=4 * 2**20),
    )(plan, ahead, behind)


SOURCE, TARGET, OWN, ENDS, FIRST = 0, HELD + 1, 2 * (HELD + 1), 3 * (HELD + 1), 4 * (HELD + 1)
COUNT, TOO_MANY, ORDER = 5 * (HELD + 1), 5 * (HELD + 1) + 1, (6 * (HELD + 1), 7 * (HELD + 1))
LISTED = 8 * (HELD + 1)


def routes():
    return [(h if side == 0 else RING - h, h, side) for h in range(1, HOPS + 1) for side in (0, 1)]


def list_kernel(chips, per, here, held, asked, plan, wanted):
    bal, core = here[0], here[1]
    slots, sources = held.shape[1] - 2 * per, held.shape[1] - per
    for device in range(RING):

        def look(j, carry, device=device):
            s = held[device, slots + j]
            wanted[device, j] = asked[s >> 1, 2 * device + (s & 1)]
            return carry

        lax.fori_loop(0, per, look, 0, unroll=8)

    def clear(k, carry):
        plan[SOURCE + k] = 0
        return carry

    lax.fori_loop(0, HELD + 1, clear, 0)

    def sender(row):
        return (bal - row + RING) & (RING - 1)

    def note(k, row, j):
        at = jnp.minimum(k, HELD)
        group = held[sender(row), slots + j] >> 1
        plan[SOURCE + at] = (bal - held[sender(row), sources + j] + RING) & (RING - 1)
        plan[TARGET + at] = (group >> 1) + chips * ((group & 1) ^ core)
        plan[OWN + at] = j

    def way(row, j):
        return (wanted[sender(row), j] - bal + row + RING) & (RING - 1)

    def own(j, k):
        note(k, 0, j)
        return k + (way(0, j) == 0).astype(jnp.int32)

    total = lax.fori_loop(0, per, own, jnp.int32(0), unroll=8)
    plan[ENDS] = jnp.minimum(total, HELD)
    plan[FIRST] = 0
    too_many = jnp.int32(0)
    index = 1
    for row, hops, side in routes():

        def one(j, carry, row=row, hops=hops, side=side):
            k, farther, opposite = carry
            d = way(row, j)
            note(k, row, j)
            is_opposite = d == HOPS
            if hops == HOPS:
                mine = is_opposite & ((opposite & 1) == side)
                far = jnp.int32(0)
            else:
                mine = d == row
                if side == 0:
                    far = ((d > row) & (d < HOPS)).astype(jnp.int32)
                else:
                    far = ((d < row) & (d > HOPS)).astype(jnp.int32)
            return (
                k + mine.astype(jnp.int32),
                farther + far,
                opposite + is_opposite.astype(jnp.int32),
            )

        stop, farther, opposite = lax.fori_loop(
            0, per, one, (total, jnp.int32(0), jnp.int32(0)), unroll=8
        )
        if hops > 1:
            if hops < HOPS:
                farther = farther + ((opposite + 1 - side) >> 1)
            first, last, limit = farther, farther + stop - total, CAPS[hops - 2]
            too_many = jnp.where(last > limit, 1, too_many)
            stop = total + jnp.minimum(last, limit) - jnp.minimum(first, limit)
            plan[FIRST + index] = first
        total = stop
        plan[ENDS + index] = jnp.minimum(total, HELD)
        index += 1
    plan[COUNT] = jnp.minimum(total, HELD)
    plan[TOO_MANY] = jnp.where(total > HELD, 1, too_many)

    def pad(k, carry):
        plan[TARGET + k] = 2 * chips
        return carry

    lax.fori_loop(jnp.minimum(total, HELD), HELD + 1, pad, 0)

    for side in range(2):
        row = 1 if side == 0 else RING - 1

        def hops_of(j, turn, side=side, row=row):
            d = way(row, j)
            is_opposite = d == HOPS
            ahead = jnp.where(is_opposite, jnp.where(turn == 0, HOPS, 0), jnp.where(d < HOPS, d, 0))
            behind = jnp.where(
                is_opposite, jnp.where(turn == 1, HOPS, 0), jnp.where(d > HOPS, RING - d, 0)
            )
            return (behind if side else ahead), turn ^ is_opposite.astype(jnp.int32)

        def count(j, carry, hops_of=hops_of):
            four, three, turn = carry
            hops, turn = hops_of(j, turn)
            return four + (hops == 4).astype(jnp.int32), three + (hops == 3).astype(jnp.int32), turn

        zero = jnp.int32(0)
        four, three, _ = lax.fori_loop(0, per, count, (zero, zero, zero), unroll=8)

        def clear_order(k, carry, side=side):
            plan[ORDER[side] + k] = 0
            return carry

        lax.fori_loop(0, per, clear_order, 0, unroll=8)

        def place(j, carry, side=side, hops_of=hops_of):
            at4, at3, at2, turn = carry
            hops, turn = hops_of(j, turn)
            where = jnp.where(
                hops == 4, at4, jnp.where(hops == 3, at3, jnp.where(hops == 2, at2, per))
            )
            plan[ORDER[side] + where] = j
            return (
                at4 + (hops == 4).astype(jnp.int32),
                at3 + (hops == 3).astype(jnp.int32),
                at2 + (hops == 2).astype(jnp.int32),
                turn,
            )

        lax.fori_loop(0, per, place, (zero, four, four + three, zero), unroll=8)


def make_list(chips, per, here, held, asked):
    smem = pl.BlockSpec(memory_space=pltpu.SMEM)
    return pl.pallas_call(
        functools.partial(list_kernel, chips, per),
        out_shape=jax.ShapeDtypeStruct((LISTED,), jnp.int32),
        in_specs=[smem] * 3,
        out_specs=smem,
        scratch_shapes=[pltpu.SMEM((RING, per), jnp.int32)],
    )(here, held, asked)


def collect_kernel(begun, plan, *refs):
    buffers, (out, held, sems) = refs[: -3 - (begun > 0)], refs[-3:]

    def copy(buffer, k, where):
        return pltpu.make_async_copy(buffer.at[where], held.at[k], sems.at[k])

    def start_of(i):
        return plan[ENDS + i - 1] if i else 0

    for i, buffer in enumerate(buffers, begun):
        start = start_of(i)

        def begin(k, carry, i=i, buffer=buffer, start=start):
            copy(buffer, k, plan[OWN + k] if i < 3 else plan[FIRST + i] + k - start).start()
            return carry

        lax.fori_loop(start, plan[ENDS + i], begin, 0)

    def finish(k, carry):
        copy(buffers[0], k, 0).wait()
        high, low = split(held[k])
        out[k] = jnp.concatenate([high, low], axis=1)
        return carry

    lax.fori_loop(start_of(begun), plan[ENDS + begun + len(buffers) - 1], finish, 0)


def collect(plan, begun, buffers, tiles=None):
    smem = pl.BlockSpec(memory_space=pltpu.SMEM)
    vmem = pl.BlockSpec(memory_space=pltpu.VMEM)
    operands = [plan] + list(buffers) + ([] if tiles is None else [tiles])
    return pl.pallas_call(
        functools.partial(collect_kernel, begun),
        out_shape=jax.ShapeDtypeStruct((HELD, BLK, 2 * BLK), jnp.bfloat16),
        in_specs=[smem]
        + [pl.BlockSpec(memory_space=pl.ANY)] * len(buffers)
        + ([] if tiles is None else [vmem]),
        out_specs=vmem,
        input_output_aliases={} if tiles is None else {len(operands) - 1: 0},
        scratch_shapes=[
            pltpu.VMEM((HELD, BLK, BLK), jnp.float32),
            pltpu.SemaphoreType.DMA((HELD,)),
        ],
        compiler_params=pltpu.CompilerParams(vmem_limit_bytes=6 * 2**20),
    )(*operands)


def products_kernel(plan, *refs):
    n_blocks = len(refs) - 3
    blocks = refs[:n_blocks]
    tiles, out, rhs = refs[n_blocks:]
    for i, block in enumerate(blocks):
        high, low = split(block[0:BLK])
        rhs[i, 0:BLK] = high
        rhs[i, BLK : 2 * BLK] = high
        rhs[i, 2 * BLK : 3 * BLK] = low
    out[...] = jnp.zeros_like(out)

    def body(turn, carry):
        first = turn * UNROLL
        found = []
        for k in range(UNROLL):
            tile = tiles[first + k]
            lhs = jnp.concatenate([tile, tile[:, :BLK]], axis=1)
            found.append(
                jnp.dot(lhs, rhs[plan[SOURCE + first + k]], preferred_element_type=jnp.float32)
            )
        for k in range(UNROLL):
            rows = pl.ds(pl.multiple_of(plan[TARGET + first + k] * BLK, BLK), BLK)
            out[rows] += found[k]
        return carry

    lax.fori_loop(0, lax.div(plan[COUNT] + (UNROLL - 1), UNROLL), body, 0)


def products(plan, blocks, tiles, n_out):
    width = blocks[0].shape[1]
    smem = pl.BlockSpec(memory_space=pltpu.SMEM)
    vmem = pl.BlockSpec(memory_space=pltpu.VMEM)
    return pl.pallas_call(
        products_kernel,
        out_shape=jax.ShapeDtypeStruct(((n_out + 1) * BLK, width), jnp.float32),
        in_specs=[smem] + [vmem] * len(blocks) + [vmem],
        out_specs=vmem,
        scratch_shapes=[pltpu.VMEM((len(blocks), 3 * BLK, width), jnp.bfloat16)],
        compiler_params=pltpu.CompilerParams(vmem_limit_bytes=6 * 2**20),
        cost_estimate=pl.CostEstimate(
            flops=32 * 3 * 2 * BLK * BLK * width, bytes_accessed=8 * 2**20, transcendentals=0
        ),
    )(plan, *blocks, tiles)


def shift(value, axis, by):
    n = lax.axis_size(axis)
    return lax.ppermute(value, axis, [(i, (i + by) % n) for i in range(n)])


def ring_hop(found, hop):
    n = lax.axis_size("bal")
    found[hop] = shift(found[hop - 1], "bal", 1)
    if n - hop > hop:
        found[n - hop] = shift(found[(n - hop + 1) % n], "bal", -1)


def ring_gather(value):
    found = {0: value}
    ring_hop(found, 1)
    found[HOPS] = shift(value, "bal", HOPS)
    for hop in range(2, HOPS):
        ring_hop(found, hop)
    return [found[h] for h in range(RING)]


def spread(value, axes):
    return lax.all_to_all(value, axes, split_axis=0, concat_axis=0, tiled=True)


def summed_everywhere(term):
    rows, width = term.shape
    half = rows // 2
    core = lax.axis_index("core")
    mine = lax.dynamic_slice_in_dim(term, core * half, half, 0)
    other = lax.dynamic_slice_in_dim(term, (1 - core) * half, half, 0)
    mine = mine + shift(other, "core", 1)
    chips = ("y", "x", "bal")
    n = lax.axis_size(chips)
    row = spread(mine, chips).reshape(n, half // n, width).sum(0)
    back = jnp.broadcast_to(row[None], (n, half // n, width)).reshape(half, width)
    mine = spread(back, chips)
    other = shift(mine, "core", 1)
    first = jnp.where(core == 0, mine, other)
    second = jnp.where(core == 0, other, mine)
    return jnp.concatenate([first, second], axis=0)


def over_the_links(
    grad_out, deriv_mask, weight, zcache, tile_values, tile_source, tile_slot, recv_target
):
    rows, width = grad_out.shape
    per_group = lax.axis_size("bal")
    slots = recv_target.shape[0]
    selector = (recv_target[:, None] == jnp.arange(per_group, dtype=jnp.int32)[None, :]).astype(
        jnp.float32
    )
    mask_float = deriv_mask.astype(jnp.float32)
    fixed_grad = grad_out
    for step in range(STEPS):
        group_rows = lax.all_gather(fixed_grad, "bal", axis=0, tiled=True)
        blocks = group_rows.reshape(per_group, BLK, width)
        partial_value = jnp.einsum(
            "tij,tjf->tif", tile_values, blocks[tile_source], precision=HIGHEST
        )
        outgoing = jnp.zeros((slots, BLK, width), jnp.float32).at[tile_slot].set(partial_value)
        incoming = spread(outgoing, GRP)
        sums = jnp.einsum("st,sif->tif", selector, incoming, precision=HIGHEST)
        owned = lax.psum_scatter(sums, "bal", scatter_dimension=0, tiled=True).reshape(rows, width)
        product = jnp.dot(owned, weight, precision=HIGHEST, preferred_element_type=jnp.float32)
        fixed_grad = mask_float * product + grad_out
    local_term = jnp.dot(
        fixed_grad.T, zcache, precision=HIGHEST, preferred_element_type=jnp.float32
    )
    return (lax.psum(local_term, ALL), fixed_grad)


def per_device(
    grad_out, deriv_mask, weight, zcache, tile_values, tile_source, tile_slot, recv_target
):
    rows, width = grad_out.shape
    n_bal = lax.axis_size("bal")
    chips = lax.axis_size(PLANE)
    bal = lax.axis_index("bal")
    core = lax.axis_index("core")
    per = tile_slot.shape[0]

    def hop(pair, size=None):
        part = slice(None) if size is None else slice(size)
        return [shift(pair[0][part], "bal", 1), shift(pair[1][part], "bal", -1)]

    blocks = {0: grad_out}
    ring_hop(blocks, 1)
    held = jnp.concatenate([recv_target, tile_slot, tile_source])
    held = spread(jnp.broadcast_to(held[None], (n_bal,) + held.shape), "bal")
    tile_values, held, blocks = lax.optimization_barrier((tile_values, held, blocks))
    came1 = hop([tile_values, tile_values])
    ring_hop(blocks, 2)
    slots = recv_target.shape[0]
    n_grp = lax.axis_size(GRP)
    asked = held[:, :slots].reshape(n_bal, n_grp, -1).transpose(1, 0, 2).reshape(n_grp, -1)
    asked = spread(jnp.pad(asked, ((0, 0), (0, BLK - asked.shape[1]))), GRP)
    plan = make_list(chips, per, jnp.stack([bal, core]), held, asked)
    came1, blocks, plan = lax.optimization_barrier((came1, blocks, plan))
    came2 = hop(pack(plan, *came1))
    ring_hop(blocks, 3)
    tiles = collect(plan, 0, [tile_values] + came1)
    came2, blocks, tiles = lax.optimization_barrier((came2, blocks, tiles))
    came3 = hop(came2, CAPS[1])
    ring_hop(blocks, 4)
    tiles = collect(plan, 3, came2, tiles)
    came3, blocks, tiles = lax.optimization_barrier((came3, blocks, tiles))
    came4 = hop(came3, CAPS[2])
    tiles = collect(plan, 5, came3, tiles)
    tiles = collect(plan, 7, came4, tiles)
    blocks = [blocks[h] for h in range(RING)]

    mask_float = deriv_mask.astype(jnp.float32)
    fixed_grad = grad_out
    half = chips * rows
    for step in range(STEPS):
        if step:
            blocks = ring_gather(fixed_grad)
        sums = products(plan, blocks, tiles, 2 * chips)
        partial_sum = sums[:half] + shift(sums[half : 2 * half], "core", 1)
        owned = spread(partial_sum, PLANE).reshape(chips, rows, width).sum(0)
        product = jnp.dot(owned, weight, precision=HIGHEST, preferred_element_type=jnp.float32)
        fixed_grad = mask_float * product + grad_out
    local_term = jnp.dot(
        fixed_grad.T, zcache, precision=HIGHEST, preferred_element_type=jnp.float32
    )
    weight_grad = summed_everywhere(jnp.where(plan[TOO_MANY] > 0, jnp.nan, local_term))
    return lax.cond(
        jnp.isnan(weight_grad[0, 0]),
        over_the_links,
        lambda *arguments: (weight_grad, fixed_grad),
        grad_out, deriv_mask, weight, zcache, tile_values, tile_source, tile_slot, recv_target,
    )


def solution(mesh):
    fine = Mesh(mesh.devices.reshape(4, 4, 2, mesh.shape["bal"]), ALL)
    in_specs = (
        P(ALL, None),
        P(ALL, None),
        P(),
        P(ALL, None),
        P(ALL, None, None),
        P(ALL),
        P(ALL),
        P(ALL),
    )
    out_specs = (P(), P(ALL, None))
    return jax.shard_map(
        per_device, mesh=fine, in_specs=in_specs, out_specs=out_specs, check_vma=False
    )
```

```python
import functools

import jax
import jax.numpy as jnp
from jax import lax
from jax.experimental import pallas as pl
from jax.experimental.pallas import tpu as pltpu
from jax.sharding import Mesh
from jax.sharding import PartitionSpec as P

STEPS = 3
BLK = 128
UNROLL = 8
RING, HOPS = 8, 4
CAPS = (22, 16, 7)
HELD = 64
PLANE = ("y", "x")
GRP = ("y", "x", "core")
ALL = ("y", "x", "core", "bal")
HIGHEST = lax.Precision.HIGHEST


def split(value):
    high = value.astype(jnp.bfloat16)
    low = (value - high.astype(jnp.float32)).astype(jnp.bfloat16)
    return high, low


def pack_kernel(plan, ahead, behind, *refs):
    outs, sems = refs[:-1], refs[-1]
    copies = []
    for side, (tiles, out) in enumerate(zip((ahead, behind), outs)):
        for k in range(CAPS[0]):
            copies.append(
                pltpu.make_async_copy(
                    tiles.at[plan[ORDER[side] + k]], out.at[k], sems.at[side * CAPS[0] + k]
                )
            )
    for copy in copies:
        copy.start()
    for copy in copies:
        copy.wait()


def pack(plan, ahead, behind):
    vmem = pl.BlockSpec(memory_space=pltpu.VMEM)
    out = jax.ShapeDtypeStruct((CAPS[0],) + ahead.shape[1:], jnp.float32)
    return pl.pallas_call(
        pack_kernel,
        out_shape=(out, out),
        in_specs=[pl.BlockSpec(memory_space=pltpu.SMEM)] + [pl.BlockSpec(memory_space=pl.ANY)] * 2,
        out_specs=(vmem, vmem),
        scratch_shapes=[pltpu.SemaphoreType.DMA((2 * CAPS[0],))],
        compiler_params=pltpu.CompilerParams(vmem_limit_bytes=4 * 2**20),
    )(plan, ahead, behind)


SOURCE, TARGET, OWN, ENDS, FIRST = 0, HELD + 1, 2 * (HELD + 1), 3 * (HELD + 1), 4 * (HELD + 1)
COUNT, TOO_MANY, ORDER = 5 * (HELD + 1), 5 * (HELD + 1) + 1, (6 * (HELD + 1), 7 * (HELD + 1))
LISTED = 8 * (HELD + 1)


def routes():
    return [(h if side == 0 else RING - h, h, side) for h in range(1, HOPS + 1) for side in (0, 1)]


def list_kernel(chips, per, here, held, asked, plan, wanted):
    bal, core = here[0], here[1]
    slots, sources = held.shape[1] - 2 * per, held.shape[1] - per
    for device in range(RING):

        def look(j, carry, device=device):
            s = held[device, slots + j]
            wanted[device, j] = asked[s >> 1, 2 * device + (s & 1)]
            return carry

        lax.fori_loop(0, per, look, 0, unroll=8)

    def clear(k, carry):
        plan[SOURCE + k] = 0
        return carry

    lax.fori_loop(0, HELD + 1, clear, 0)

    def sender(row):
        return (bal - row + RING) & (RING - 1)

    def note(k, row, j):
        at = jnp.minimum(k, HELD)
        group = held[sender(row), slots + j] >> 1
        plan[SOURCE + at] = (bal - held[sender(row), sources + j] + RING) & (RING - 1)
        plan[TARGET + at] = (group >> 1) + chips * ((group & 1) ^ core)
        plan[OWN + at] = j

    def way(row, j):
        return (wanted[sender(row), j] - bal + row + RING) & (RING - 1)

    def own(j, k):
        note(k, 0, j)
        return k + (way(0, j) == 0).astype(jnp.int32)

    total = lax.fori_loop(0, per, own, jnp.int32(0), unroll=8)
    plan[ENDS] = jnp.minimum(total, HELD)
    plan[FIRST] = 0
    too_many = jnp.int32(0)
    index = 1
    for row, hops, side in routes():

        def one(j, carry, row=row, hops=hops, side=side):
            k, farther, opposite = carry
            d = way(row, j)
            note(k, row, j)
            is_opposite = d == HOPS
            if hops == HOPS:
                mine = is_opposite & ((opposite & 1) == side)
                far = jnp.int32(0)
            else:
                mine = d == row
                if side == 0:
                    far = ((d > row) & (d < HOPS)).astype(jnp.int32)
                else:
                    far = ((d < row) & (d > HOPS)).astype(jnp.int32)
            return (
                k + mine.astype(jnp.int32),
                farther + far,
                opposite + is_opposite.astype(jnp.int32),
            )

        stop, farther, opposite = lax.fori_loop(
            0, per, one, (total, jnp.int32(0), jnp.int32(0)), unroll=8
        )
        if hops > 1:
            if hops < HOPS:
                farther = farther + ((opposite + 1 - side) >> 1)
            first, last, limit = farther, farther + stop - total, CAPS[hops - 2]
            too_many = jnp.where(last > limit, 1, too_many)
            stop = total + jnp.minimum(last, limit) - jnp.minimum(first, limit)
            plan[FIRST + index] = first
        total = stop
        plan[ENDS + index] = jnp.minimum(total, HELD)
        index += 1
    plan[COUNT] = jnp.minimum(total, HELD)
    plan[TOO_MANY] = jnp.where(total > HELD, 1, too_many)

    def pad(k, carry):
        plan[TARGET + k] = 2 * chips
        return carry

    lax.fori_loop(jnp.minimum(total, HELD), HELD + 1, pad, 0)

    for side in range(2):
        row = 1 if side == 0 else RING - 1

        def hops_of(j, turn, side=side, row=row):
            d = way(row, j)
            is_opposite = d == HOPS
            ahead = jnp.where(is_opposite, jnp.where(turn == 0, HOPS, 0), jnp.where(d < HOPS, d, 0))
            behind = jnp.where(
                is_opposite, jnp.where(turn == 1, HOPS, 0), jnp.where(d > HOPS, RING - d, 0)
            )
            return (behind if side else ahead), turn ^ is_opposite.astype(jnp.int32)

        def count(j, carry, hops_of=hops_of):
            four, three, turn = carry
            hops, turn = hops_of(j, turn)
            return four + (hops == 4).astype(jnp.int32), three + (hops == 3).astype(jnp.int32), turn

        zero = jnp.int32(0)
        four, three, _ = lax.fori_loop(0, per, count, (zero, zero, zero), unroll=8)

        def clear_order(k, carry, side=side):
            plan[ORDER[side] + k] = 0
            return carry

        lax.fori_loop(0, per, clear_order, 0, unroll=8)

        def place(j, carry, side=side, hops_of=hops_of):
            at4, at3, at2, turn = carry
            hops, turn = hops_of(j, turn)
            where = jnp.where(
                hops == 4, at4, jnp.where(hops == 3, at3, jnp.where(hops == 2, at2, per))
            )
            plan[ORDER[side] + where] = j
            return (
                at4 + (hops == 4).astype(jnp.int32),
                at3 + (hops == 3).astype(jnp.int32),
                at2 + (hops == 2).astype(jnp.int32),
                turn,
            )

        lax.fori_loop(0, per, place, (zero, four, four + three, zero), unroll=8)


def make_list(chips, per, here, held, asked):
    smem = pl.BlockSpec(memory_space=pltpu.SMEM)
    return pl.pallas_call(
        functools.partial(list_kernel, chips, per),
        out_shape=jax.ShapeDtypeStruct((LISTED,), jnp.int32),
        in_specs=[smem] * 3,
        out_specs=smem,
        scratch_shapes=[pltpu.SMEM((RING, per), jnp.int32)],
    )(here, held, asked)


def collect_kernel(begun, plan, *refs):
    buffers, (out, held, packed, sems, out_sems) = refs[: -5 - (begun > 0)], refs[-5:]

    def copy(buffer, k, where):
        return pltpu.make_async_copy(buffer.at[where], held.at[k], sems.at[k])

    def start_of(i):
        return plan[ENDS + i - 1] if i else 0

    for i, buffer in enumerate(buffers, begun):
        start = start_of(i)

        def begin(k, carry, i=i, buffer=buffer, start=start):
            copy(buffer, k, plan[OWN + k] if i < 3 else plan[FIRST + i] + k - start).start()
            return carry

        lax.fori_loop(start, plan[ENDS + i], begin, 0)

    def finish(k, carry):
        copy(buffers[0], k, 0).wait()
        high, low = split(held[k])
        packed[k] = jnp.concatenate([high, low], axis=1)
        hand_over(k).start()
        return carry

    def hand_over(k):
        return pltpu.make_async_copy(packed.at[k], out.at[k], out_sems.at[k])

    def settle(k, carry):
        hand_over(k).wait()
        return carry

    first, last = start_of(begun), plan[ENDS + begun + len(buffers) - 1]
    lax.fori_loop(first, last, finish, 0)
    lax.fori_loop(first, last, settle, 0)


def collect(plan, begun, buffers, tiles=None):
    smem = pl.BlockSpec(memory_space=pltpu.SMEM)
    hbm = pl.BlockSpec(memory_space=pltpu.HBM)
    operands = [plan] + list(buffers) + ([] if tiles is None else [tiles])
    return pl.pallas_call(
        functools.partial(collect_kernel, begun),
        out_shape=jax.ShapeDtypeStruct((HELD, BLK, 2 * BLK), jnp.bfloat16),
        in_specs=[smem]
        + [pl.BlockSpec(memory_space=pl.ANY)] * len(buffers)
        + ([] if tiles is None else [hbm]),
        out_specs=hbm,
        input_output_aliases={} if tiles is None else {len(operands) - 1: 0},
        scratch_shapes=[
            pltpu.VMEM((HELD, BLK, BLK), jnp.float32),
            pltpu.VMEM((HELD, BLK, 2 * BLK), jnp.bfloat16),
            pltpu.SemaphoreType.DMA((HELD,)),
            pltpu.SemaphoreType.DMA((HELD,)),
        ],
        compiler_params=pltpu.CompilerParams(vmem_limit_bytes=12 * 2**20),
    )(*operands)


def products_kernel(plan, *refs):
    n_blocks = len(refs) - 5
    blocks = refs[:n_blocks]
    tiles, out, rhs, held, sems = refs[n_blocks:]
    turns = lax.div(plan[COUNT] + (UNROLL - 1), UNROLL)

    def copy(turn):
        part = pl.ds(turn * UNROLL, UNROLL)
        return pltpu.make_async_copy(tiles.at[part], held.at[part], sems.at[turn])

    def begin(turn, carry):
        copy(turn).start()
        return carry

    lax.fori_loop(0, turns, begin, 0)
    for i, block in enumerate(blocks):
        high, low = split(block[0:BLK])
        rhs[i, 0:BLK] = high
        rhs[i, BLK : 2 * BLK] = high
        rhs[i, 2 * BLK : 3 * BLK] = low
    out[...] = jnp.zeros_like(out)

    def body(turn, carry):
        first = turn * UNROLL
        copy(turn).wait()
        found = []
        for k in range(UNROLL):
            tile = held[first + k]
            lhs = jnp.concatenate([tile, tile[:, :BLK]], axis=1)
            found.append(
                jnp.dot(lhs, rhs[plan[SOURCE + first + k]], preferred_element_type=jnp.float32)
            )
        for k in range(UNROLL):
            rows = pl.ds(pl.multiple_of(plan[TARGET + first + k] * BLK, BLK), BLK)
            out[rows] += found[k]
        return carry

    lax.fori_loop(0, turns, body, 0)


def products(plan, blocks, tiles, n_out):
    width = blocks[0].shape[1]
    smem = pl.BlockSpec(memory_space=pltpu.SMEM)
    vmem = pl.BlockSpec(memory_space=pltpu.VMEM)
    return pl.pallas_call(
        products_kernel,
        out_shape=jax.ShapeDtypeStruct(((n_out + 1) * BLK, width), jnp.float32),
        in_specs=[smem] + [vmem] * len(blocks) + [pl.BlockSpec(memory_space=pltpu.HBM)],
        out_specs=vmem,
        scratch_shapes=[
            pltpu.VMEM((len(blocks), 3 * BLK, width), jnp.bfloat16),
            pltpu.VMEM((HELD, BLK, 2 * BLK), jnp.bfloat16),
            pltpu.SemaphoreType.DMA((HELD // UNROLL,)),
        ],
        compiler_params=pltpu.CompilerParams(vmem_limit_bytes=12 * 2**20),
        cost_estimate=pl.CostEstimate(
            flops=32 * 3 * 2 * BLK * BLK * width, bytes_accessed=8 * 2**20, transcendentals=0
        ),
    )(plan, *blocks, tiles)


def shift(value, axis, by):
    n = lax.axis_size(axis)
    return lax.ppermute(value, axis, [(i, (i + by) % n) for i in range(n)])


def ring_hop(found, hop):
    n = lax.axis_size("bal")
    found[hop] = shift(found[hop - 1], "bal", 1)
    if n - hop > hop:
        found[n - hop] = shift(found[(n - hop + 1) % n], "bal", -1)


def ring_gather(value):
    found = {0: value}
    ring_hop(found, 1)
    found[HOPS] = shift(value, "bal", HOPS)
    for hop in range(2, HOPS):
        ring_hop(found, hop)
    return [found[h] for h in range(RING)]


def spread(value, axes):
    return lax.all_to_all(value, axes, split_axis=0, concat_axis=0, tiled=True)


def summed_everywhere(term):
    rows, width = term.shape
    half = rows // 2
    core = lax.axis_index("core")
    mine = lax.dynamic_slice_in_dim(term, core * half, half, 0)
    other = lax.dynamic_slice_in_dim(term, (1 - core) * half, half, 0)
    mine = mine + shift(other, "core", 1)
    chips = ("y", "x", "bal")
    n = lax.axis_size(chips)
    row = spread(mine, chips).reshape(n, half // n, width).sum(0)
    back = jnp.broadcast_to(row[None], (n, half // n, width)).reshape(half, width)
    mine = spread(back, chips)
    other = shift(mine, "core", 1)
    first = jnp.where(core == 0, mine, other)
    second = jnp.where(core == 0, other, mine)
    return jnp.concatenate([first, second], axis=0)


def over_the_links(
    grad_out, deriv_mask, weight, zcache, tile_values, tile_source, tile_slot, recv_target
):
    rows, width = grad_out.shape
    per_group = lax.axis_size("bal")
    slots = recv_target.shape[0]
    selector = (recv_target[:, None] == jnp.arange(per_group, dtype=jnp.int32)[None, :]).astype(
        jnp.float32
    )
    mask_float = deriv_mask.astype(jnp.float32)
    fixed_grad = grad_out
    for step in range(STEPS):
        group_rows = lax.all_gather(fixed_grad, "bal", axis=0, tiled=True)
        blocks = group_rows.reshape(per_group, BLK, width)
        partial_value = jnp.einsum(
            "tij,tjf->tif", tile_values, blocks[tile_source], precision=HIGHEST
        )
        outgoing = jnp.zeros((slots, BLK, width), jnp.float32).at[tile_slot].set(partial_value)
        incoming = spread(outgoing, GRP)
        sums = jnp.einsum("st,sif->tif", selector, incoming, precision=HIGHEST)
        owned = lax.psum_scatter(sums, "bal", scatter_dimension=0, tiled=True).reshape(rows, width)
        product = jnp.dot(owned, weight, precision=HIGHEST, preferred_element_type=jnp.float32)
        fixed_grad = mask_float * product + grad_out
    local_term = jnp.dot(
        fixed_grad.T, zcache, precision=HIGHEST, preferred_element_type=jnp.float32
    )
    return (lax.psum(local_term, ALL), fixed_grad)


def per_device(
    grad_out, deriv_mask, weight, zcache, tile_values, tile_source, tile_slot, recv_target
):
    rows, width = grad_out.shape
    n_bal = lax.axis_size("bal")
    chips = lax.axis_size(PLANE)
    bal = lax.axis_index("bal")
    core = lax.axis_index("core")
    per = tile_slot.shape[0]

    def hop(pair, size=None):
        part = slice(None) if size is None else slice(size)
        return [shift(pair[0][part], "bal", 1), shift(pair[1][part], "bal", -1)]

    blocks = {0: grad_out}
    ring_hop(blocks, 1)
    held = jnp.concatenate([recv_target, tile_slot, tile_source])
    held = spread(jnp.broadcast_to(held[None], (n_bal,) + held.shape), "bal")
    tile_values, held = lax.optimization_barrier((tile_values, held))
    came1 = hop([tile_values, tile_values])
    slots = recv_target.shape[0]
    n_grp = lax.axis_size(GRP)
    asked = held[:, :slots].reshape(n_bal, n_grp, -1).transpose(1, 0, 2).reshape(n_grp, -1)
    asked = spread(jnp.pad(asked, ((0, 0), (0, BLK - asked.shape[1]))), GRP)
    plan = make_list(chips, per, jnp.stack([bal, core]), held, asked)
    came1, blocks, plan = lax.optimization_barrier((came1, blocks, plan))
    came2 = hop(pack(plan, *came1))
    ring_hop(blocks, 2)
    tiles = collect(plan, 0, [tile_values] + came1)
    came2, blocks, tiles = lax.optimization_barrier((came2, blocks, tiles))
    came3 = hop(came2, CAPS[1])
    ring_hop(blocks, 3)
    tiles = collect(plan, 3, came2, tiles)
    came3, blocks, tiles = lax.optimization_barrier((came3, blocks, tiles))
    came4 = hop(came3, CAPS[2])
    ring_hop(blocks, 4)
    tiles = collect(plan, 5, came3, tiles)
    tiles = collect(plan, 7, came4, tiles)
    blocks = [blocks[h] for h in range(RING)]

    mask_float = deriv_mask.astype(jnp.float32)
    fixed_grad = grad_out
    half = chips * rows
    for step in range(STEPS):
        if step:
            blocks = ring_gather(fixed_grad)
        sums = products(plan, blocks, tiles, 2 * chips)
        partial_sum = sums[:half] + shift(sums[half : 2 * half], "core", 1)
        owned = spread(partial_sum, PLANE).reshape(chips, rows, width).sum(0)
        product = jnp.dot(owned, weight, precision=HIGHEST, preferred_element_type=jnp.float32)
        fixed_grad = mask_float * product + grad_out
    local_term = jnp.dot(
        fixed_grad.T, zcache, precision=HIGHEST, preferred_element_type=jnp.float32
    )
    weight_grad = summed_everywhere(jnp.where(plan[TOO_MANY] > 0, jnp.nan, local_term))
    return lax.cond(
        jnp.isnan(weight_grad[0, 0]),
        over_the_links,
        lambda *arguments: (weight_grad, fixed_grad),
        grad_out, deriv_mask, weight, zcache, tile_values, tile_source, tile_slot, recv_target,
    )


def solution(mesh):
    fine = Mesh(mesh.devices.reshape(4, 4, 2, mesh.shape["bal"]), ALL)
    in_specs = (
        P(ALL, None),
        P(ALL, None),
        P(),
        P(ALL, None),
        P(ALL, None, None),
        P(ALL),
        P(ALL),
        P(ALL),
    )
    out_specs = (P(), P(ALL, None))
    return jax.shard_map(
        per_device, mesh=fine, in_specs=in_specs, out_specs=out_specs, check_vma=False
    )
```
